128 devices in a mesh: rows: 64 (over z_lo, x, y, core), feat: 2 (over z_hi).
Axes of the slice: x: 4, y: 4, z: 4 (z_hi: 2, z_lo: 2; z = z_hi * 2 + z_lo), core: 2. Of those that a mesh axis runs over, the one named last changes fastest.
Arguments:
- cells: bfloat16 [1024, 64, 192], P('rows', 'feat'), may hold values from -6 to 6
- split: int32 [64], replicated, may hold values from 14 to 16, as said below
- w_qkv_feat: bfloat16 [192, 576], replicated, may hold values from -0.4375 to 0.4375
- w_out_feat: bfloat16 [192, 192], replicated, may hold values from -0.4375 to 0.4375
- w_qkv_samp: bfloat16 [192, 576], replicated, may hold values from -0.4375 to 0.4375
- w_out_samp: bfloat16 [192, 192], replicated, may hold values from -0.4375 to 0.4375
- w_up: bfloat16 [192, 768], replicated, may hold values from -0.4375 to 0.4375
- w_down: bfloat16 [768, 192], replicated, may hold values from -0.21875 to 0.21875
- cotangent: bfloat16 [1024, 64, 192], P('rows', 'feat'), may hold values from -6 to 6
Outputs:
- layer_out: bfloat16 [1024, 64, 192], P('rows', 'feat')
- grad_cells: bfloat16 [1024, 64, 192], P('rows', 'feat')
- grad_qkv_feat: float32 [192, 576], replicated
- grad_out_feat: float32 [192, 192], replicated
- grad_qkv_samp: float32 [192, 576], replicated
- grad_out_samp: float32 [192, 192], replicated
- grad_up: float32 [192, 768], replicated
- grad_down: float32 [768, 192], replicated
The draws below stay inside these ranges and needn't reach their ends.
Inputs may be any that keep to these rules, and one draw needn't show every extreme that they name: split[i] counts the training rows among the 16 rows of block i; they come first in the block and the rest of the block are query rows.
All inputs are finite; a program needn't handle non-finite values.
Results may differ from the reference program's by a relative error of at most 0.033.
Values may be sent and summed in bfloat16 or wider, within the bound.
No kernel may reach another device: no remote copies, remote signals or barrier semaphores. Data moves between devices by JAX's collectives and lax.ppermute only.
A program may use at most 128 MiB of HBM per device.

```python
import jax
import jax.numpy as jnp
from jax import lax

E = 192
H = 6
FF = 768
F = 64
ROWS_DEV = 16
ROWS = 1024
BLOCKS = 64


def draw_split(key, part):
    key = jax.random.fold_in(key, 7)
    key_base, key_high, key_low = jax.random.split(key, 3)
    lowest = ROWS_DEV - ROWS_DEV // 8
    counts = jax.random.randint(key_base, (BLOCKS,), lowest, ROWS_DEV + 1)
    first = jax.random.randint(key_high, (), 0, BLOCKS)
    second = (first + 1 + jax.random.randint(key_low, (), 0, BLOCKS - 1)) % BLOCKS
    counts = counts.at[first].set(ROWS_DEV).at[second].set(lowest)
    return counts.astype(jnp.int32)


def level_of(stream_key, extent, cuts, smallest, high):
    factor_of = 1.0
    for axis_at, shards_of in cuts:
        heights = jax.random.uniform(jax.random.fold_in(jax.random.fold_in(stream_key, 6), axis_at), (shards_of,), jnp.float32, smallest / len(cuts), high / len(cuts))
        factor_of = factor_of * jnp.repeat(jnp.exp(heights), extent[axis_at] // shards_of).reshape((-1,) + (1,) * (len(extent) - 1 - axis_at))
    return factor_of


def normal_values(key, shape, scale, reach, cuts=(), held_as=jnp.bfloat16):
    drawn = jax.random.normal(key, shape, jnp.float32) * scale
    if len(cuts) > 0:
        drawn = level_of(key, shape, cuts, -0.22, 0.18) * drawn
    return jnp.clip(drawn, min=-reach, max=reach).astype(held_as)


def setup_inputs(seed: int = 0) -> dict:
    splits = jax.random.split(jax.random.key(seed), 10)
    cells = normal_values(splits[0], (ROWS, F, E), 1.0, 6.0, ((0, 64), (1, 2)))
    split = draw_split(jax.random.fold_in(splits[9], 71), 0)
    w_qkv_feat = normal_values(splits[2], (E, 3 * E), E ** -0.5, 0.4375)
    w_out_feat = normal_values(splits[3], (E, E), E ** -0.5, 0.4375)
    w_qkv_samp = normal_values(splits[4], (E, 3 * E), E ** -0.5, 0.4375)
    w_out_samp = normal_values(splits[5], (E, E), E ** -0.5, 0.4375)
    w_up = normal_values(splits[6], (E, FF), E ** -0.5, 0.4375)
    w_down = normal_values(splits[7], (FF, E), FF ** -0.5, 0.21875)
    cotangent = normal_values(splits[8], (ROWS, F, E), 1.0, 6.0, ((0, 64), (1, 2)))
    return dict(cells=cells, split=split, w_qkv_feat=w_qkv_feat, w_out_feat=w_out_feat, w_qkv_samp=w_qkv_samp, w_out_samp=w_out_samp, w_up=w_up, w_down=w_down, cotangent=cotangent)


EPS = 1e-05

def layer_norm(v):
    mean = lax.optimization_barrier(jnp.mean(v, axis=-1, keepdims=True))
    centered = v - mean
    var = lax.optimization_barrier(jnp.mean(centered * centered, axis=-1, keepdims=True))
    return centered * lax.rsqrt(var + EPS)

def norm_back(v, grad):
    mean = lax.optimization_barrier(jnp.mean(v, axis=-1, keepdims=True))
    centered = v - mean
    var = lax.optimization_barrier(jnp.mean(centered * centered, axis=-1, keepdims=True))
    inv_std = lax.rsqrt(var + EPS)
    normed = centered * inv_std
    return inv_std * (grad - lax.optimization_barrier(jnp.mean(grad, axis=-1, keepdims=True)) - normed * lax.optimization_barrier(jnp.mean(grad * normed, axis=-1, keepdims=True)))

def block_probs(query_block, keys, keymask, scale):
    scores = lax.dot_general(query_block, keys, (((0,), (0,)), ((), ())), preferred_element_type=jnp.float32) * scale
    scores = jnp.where(keymask[None, :], scores, -1e+30)
    top = lax.optimization_barrier(jnp.max(scores, axis=-1, keepdims=True))
    expo = jnp.exp(scores - top)
    return expo / lax.optimization_barrier(jnp.sum(expo, axis=-1, keepdims=True))

def pair_forward(query, keys, values, keymask):
    head_dim, total = query.shape
    scale = head_dim ** (-0.5)
    block = min(512, total)
    blocks = query.reshape(head_dim, total // block, block).transpose(1, 0, 2)

    def one_block(query_block):
        probs = block_probs(query_block, keys, keymask, scale).astype(jnp.bfloat16)
        return lax.dot_general(values, probs, (((1,), (1,)), ((), ())), preferred_element_type=jnp.float32).astype(jnp.bfloat16)
    outs = lax.map(one_block, blocks)
    return outs.transpose(1, 0, 2).reshape(head_dim, total)

def pair_backward(query, keys, values, grad_out, keymask):
    head_dim, total = query.shape
    scale = head_dim ** (-0.5)
    block = min(512, total)
    query_blocks = query.reshape(head_dim, total // block, block).transpose(1, 0, 2)
    grad_blocks = grad_out.reshape(head_dim, total // block, block).transpose(1, 0, 2)

    def one_block(carry, pieces):
        query_block, grad_block = pieces
        probs = block_probs(query_block, keys, keymask, scale)
        probs_low = probs.astype(jnp.bfloat16)
        dprob = lax.dot_general(grad_block, values, (((0,), (0,)), ((), ())), preferred_element_type=jnp.float32)
        dscore = (probs * (dprob - lax.optimization_barrier(jnp.sum(probs * dprob, axis=-1, keepdims=True)))).astype(jnp.bfloat16)
        dquery = lax.dot_general(keys, dscore, (((1,), (1,)), ((), ())), preferred_element_type=jnp.float32) * scale
        dkeys = carry[0] + jnp.dot(query_block, dscore, preferred_element_type=jnp.float32) * scale
        dvalues = carry[1] + jnp.dot(grad_block, probs_low, preferred_element_type=jnp.float32)
        return ((dkeys, dvalues), dquery)
    zeros = jnp.zeros((head_dim, total), jnp.float32)
    (dkeys, dvalues), dquery = lax.scan(one_block, (zeros, zeros), (query_blocks, grad_blocks))
    return (dquery.transpose(1, 0, 2).reshape(head_dim, total), dkeys, dvalues)

def feat_probs(query, keys, scale):
    scores = jnp.einsum('rfhd,rghd->rhfg', query.astype(jnp.float32), keys.astype(jnp.float32)) * scale
    return jax.nn.softmax(scores, axis=-1)

def feat_forward(query, keys, values):
    scale = query.shape[-1] ** (-0.5)
    probs = feat_probs(query, keys, scale).astype(jnp.bfloat16)
    out = jnp.einsum('rhfg,rghd->rfhd', probs.astype(jnp.float32), values.astype(jnp.float32))
    return out.astype(jnp.bfloat16)

def feat_backward(query, keys, values, grad_out):
    scale = query.shape[-1] ** (-0.5)
    probs = feat_probs(query, keys, scale)
    probs_low = probs.astype(jnp.bfloat16).astype(jnp.float32)
    grad32 = grad_out.astype(jnp.float32)
    dprob = jnp.einsum('rfhd,rghd->rhfg', grad32, values.astype(jnp.float32))
    dscore = (probs * (dprob - lax.optimization_barrier(jnp.sum(probs * dprob, axis=-1, keepdims=True)))).astype(jnp.bfloat16).astype(jnp.float32)
    dquery = jnp.einsum('rhfg,rghd->rfhd', dscore, keys.astype(jnp.float32)) * scale
    dkeys = jnp.einsum('rhfg,rfhd->rghd', dscore, query.astype(jnp.float32)) * scale
    dvalues = jnp.einsum('rhfg,rfhd->rghd', probs_low, grad32)
    return (dquery, dkeys, dvalues)

def reference(cells, split, w_qkv_feat, w_out_feat, w_qkv_samp, w_out_samp, w_up, w_down, cotangent):
    head_dim = E // H
    flat = cells.reshape(-1, E)
    normed_a = layer_norm(flat.astype(jnp.float32)).astype(jnp.bfloat16)
    qkv_a = jnp.dot(normed_a, w_qkv_feat, preferred_element_type=jnp.float32).astype(jnp.bfloat16).reshape(ROWS, F, 3, H, head_dim)
    att_a = feat_forward(qkv_a[:, :, 0], qkv_a[:, :, 1], qkv_a[:, :, 2]).reshape(-1, E)
    mid_a = (flat.astype(jnp.float32) + jnp.dot(att_a, w_out_feat, preferred_element_type=jnp.float32)).astype(jnp.bfloat16)
    normed_b = layer_norm(mid_a.astype(jnp.float32)).astype(jnp.bfloat16)
    qkv_b = jnp.dot(normed_b, w_qkv_samp, preferred_element_type=jnp.float32).astype(jnp.bfloat16)
    columns = qkv_b.reshape(ROWS, F, 3, H, head_dim).transpose(1, 3, 2, 4, 0).reshape(F * H, 3, head_dim, ROWS)
    keymask = (jnp.arange(ROWS_DEV, dtype=jnp.int32)[None, :] < split[:, None]).reshape(-1)
    att_cols = lax.map(lambda t: pair_forward(t[0], t[1], t[2], keymask), (columns[:, 0], columns[:, 1], columns[:, 2]))
    att_b = att_cols.reshape(F, H, head_dim, ROWS).transpose(3, 0, 1, 2).reshape(-1, E)
    mid_b = (mid_a.astype(jnp.float32) + jnp.dot(att_b, w_out_samp, preferred_element_type=jnp.float32)).astype(jnp.bfloat16)
    normed_c = layer_norm(mid_b.astype(jnp.float32)).astype(jnp.bfloat16)
    pre = jnp.dot(normed_c, w_up, preferred_element_type=jnp.float32)
    hidden, gelu_back = jax.vjp(jax.nn.gelu, pre)
    hidden = hidden.astype(jnp.bfloat16)
    layer_out = (mid_b.astype(jnp.float32) + jnp.dot(hidden, w_down, preferred_element_type=jnp.float32)).astype(jnp.bfloat16)
    grad = cotangent.reshape(-1, E)
    sum_down = jnp.dot(hidden.T, grad, preferred_element_type=jnp.float32)
    d_pre = gelu_back(jnp.dot(grad, w_down.T, preferred_element_type=jnp.float32))[0].astype(jnp.bfloat16)
    sum_up = jnp.dot(normed_c.T, d_pre, preferred_element_type=jnp.float32)
    d_mid_b = (grad.astype(jnp.float32) + norm_back(mid_b.astype(jnp.float32), jnp.dot(d_pre, w_up.T, preferred_element_type=jnp.float32))).astype(jnp.bfloat16)
    sum_out_samp = jnp.dot(att_b.T, d_mid_b, preferred_element_type=jnp.float32)
    d_att_b = jnp.dot(d_mid_b, w_out_samp.T, preferred_element_type=jnp.float32).astype(jnp.bfloat16)
    d_att_cols = d_att_b.reshape(ROWS, F, H, head_dim).transpose(1, 2, 3, 0).reshape(F * H, head_dim, ROWS)
    d_query, d_keys, d_values = lax.map(lambda t: pair_backward(t[0], t[1], t[2], t[3], keymask), (columns[:, 0], columns[:, 1], columns[:, 2], d_att_cols))
    d_cols = jnp.stack((d_query, d_keys, d_values), axis=1).astype(jnp.bfloat16)
    d_qkv_b = d_cols.reshape(F, H, 3, head_dim, ROWS).transpose(4, 0, 2, 1, 3).reshape(-1, 3 * E)
    sum_qkv_samp = jnp.dot(normed_b.T, d_qkv_b, preferred_element_type=jnp.float32)
    d_mid_a = (d_mid_b.astype(jnp.float32) + norm_back(mid_a.astype(jnp.float32), jnp.dot(d_qkv_b, w_qkv_samp.T, preferred_element_type=jnp.float32))).astype(jnp.bfloat16)
    sum_out_feat = jnp.dot(att_a.T, d_mid_a, preferred_element_type=jnp.float32)
    d_att_a = jnp.dot(d_mid_a, w_out_feat.T, preferred_element_type=jnp.float32).astype(jnp.bfloat16).reshape(ROWS, F, H, head_dim)
    dq_a, dk_a, dv_a = feat_backward(qkv_a[:, :, 0], qkv_a[:, :, 1], qkv_a[:, :, 2], d_att_a)
    d_qkv_a = jnp.stack((dq_a, dk_a, dv_a), axis=2).astype(jnp.bfloat16).reshape(-1, 3 * E)
    sum_qkv_feat = jnp.dot(normed_a.T, d_qkv_a, preferred_element_type=jnp.float32)
    grad_cells = (d_mid_a.astype(jnp.float32) + norm_back(flat.astype(jnp.float32), jnp.dot(d_qkv_a, w_qkv_feat.T, preferred_element_type=jnp.float32))).astype(jnp.bfloat16)
    factor = (ROWS * F) ** (-0.5)
    return (layer_out.reshape(ROWS, F, E), grad_cells.reshape(ROWS, F, E), sum_qkv_feat * factor, sum_out_feat * factor, sum_qkv_samp * factor, sum_out_samp * factor, sum_up * factor, sum_down * factor)
```

```python
import jax
import jax.numpy as jnp
from jax import lax
from jax.experimental import pallas as pl
from jax.experimental.pallas import tpu as pltpu
from jax.sharding import Mesh, PartitionSpec as P

H = 6
D = 32
E = 192
EPS = 1e-05
SCALE = D ** -0.5
EXP2_SCALE = SCALE * 1.4426950408889634
NEG = -1e30
GELU_A = 0.7978845608028654
GELU_B = 0.044715
f32 = jnp.float32
bf16 = jnp.bfloat16
EARLY_ROWS = 4096
LATE_ROWS = 2048


def dot(a, b):
    return jnp.dot(a, b, preferred_element_type=f32)


def dot_nt(a, b):
    return lax.dot_general(a, b, (((1,), (1,)), ((), ())), preferred_element_type=f32)


def transposed(v):
    return jnp.transpose(v.astype(f32))


def norm(v):
    centered = v - jnp.mean(v, axis=-1, keepdims=True)
    inv_std = lax.rsqrt(jnp.mean(centered * centered, axis=-1, keepdims=True) + EPS)
    return centered * inv_std, inv_std


def norm_back(normed, inv_std, grad):
    return inv_std * (
        grad
        - jnp.mean(grad, axis=-1, keepdims=True)
        - normed * jnp.mean(grad * normed, axis=-1, keepdims=True)
    )


def place(rows, head, extra):
    count = rows.shape[1]
    parts = []
    if head > 0:
        parts.append(jnp.zeros((D * head, count), bf16))
    parts.append(rows)
    if head < H - 1:
        parts.append(jnp.zeros((E - D * (head + 1), count), bf16))
    parts.append(extra)
    return jnp.concatenate(parts, axis=0)


def split_rows(delta):
    high = (-delta).astype(bf16).astype(f32)
    low = -delta - high
    at = lax.broadcasted_iota(jnp.int32, (16, delta.shape[1]), 0)
    return jnp.where(at == 0, high, jnp.where(at == 1, low, 0.0)).astype(bf16)


def pack_tiles(q, k, v, out):
    lane = lax.broadcasted_iota(jnp.int32, (E, 128), 1)
    roll = lambda t: pltpu.roll(t, 64, 1)
    low = lane < 64
    return (
        q[:, :128],
        jnp.where(low, q[:, 128:], roll(k[:, :128])),
        jnp.where(low, roll(k[:, :128]), roll(k[:, 128:])),
        v[:, :128],
        out[:, :128],
        jnp.where(low, v[:, 128:], roll(out[:, 128:])),
    )


def unpack_tiles(tile, qkv_ref, out_ref, factor):
    for t in range(4):
        qkv_ref[:, 128 * t : 128 * (t + 1)] = tile(t) * factor
    last = tile(5) * factor
    qkv_ref[:, 512:576] = last[:, :64]
    out_ref[:, :128] = tile(4) * factor
    out_ref[:, 128:192] = pltpu.roll(last, 64, 1)[:, :64]


def pad_lanes(v):
    return jnp.concatenate([v, jnp.zeros((v.shape[0], 256 - E), v.dtype)], axis=1)


def row_forward(
    zhi_ref, cells_ref, recv_ref, wpad_ref, wt_ref, wout_ref,
    mid_ref, x_ref, na_ref, qt_ref, kt_ref, va_ref, e_ref, inv_ref, ot_ref,
    x_scr, t_scr,
):
    zhi = zhi_ref[0]
    for r in range(8):
        mine = pl.multiple_of(64 * r + 32 * zhi, 32)
        other = pl.multiple_of(64 * r + 32 * (1 - zhi), 32)
        src = pl.multiple_of(256 * zhi + 32 * r, 32)
        x_scr[pl.ds(mine, 32), :] = cells_ref[pl.ds(src, 32), :].astype(f32)
        x_scr[pl.ds(other, 32), :] = recv_ref[32 * r : 32 * (r + 1), :].astype(f32)
    x = x_scr[...]
    x_ref[...] = x.astype(bf16)
    normed, _ = norm(x)
    na = normed.astype(bf16)
    na_ref[...] = na
    qkv_t = dot_nt(wt_ref[...], na).astype(bf16)
    qt_ref[...] = qkv_t[:E]
    kt_ref[...] = qkv_t[E : 2 * E]
    vt = qkv_t[2 * E :]
    lane = lax.broadcasted_iota(jnp.int32, (512, 256), 1)
    row = lax.broadcasted_iota(jnp.int32, (512, 256), 0)
    odd = (row // 64) % 2
    flags = jnp.where((lane == E) & (odd == 0), 1.0, jnp.where((lane == E + 1) & (odd == 1), 1.0, 0.0))
    ka = (dot(na, wpad_ref[:, 256:512]) + flags).astype(bf16)
    ones = jnp.where((lane == E) | (lane == E + 1), 1.0, 0.0)
    va_ref[...] = (dot(na, wpad_ref[:, 512:768]) + ones).astype(bf16)
    at = lax.broadcasted_iota(jnp.int32, (16, 128), 0)
    col = lax.broadcasted_iota(jnp.int32, (16, 128), 1)
    other_row = ((at == 0) & (col >= 64)) | ((at == 1) & (col < 64))
    extra = jnp.where(other_row, NEG, 0.0).astype(bf16)
    one_rows = jnp.ones((16, 128), bf16)
    for p in range(4):
        cols = slice(128 * p, 128 * (p + 1))
        rhs = jnp.concatenate(
            [place(qkv_t[D * h : D * (h + 1), cols], h, extra) for h in range(H)], axis=1
        )
        scores = dot(ka[cols, : E + 16], rhs)
        top = jnp.max(scores, axis=0, keepdims=True)
        e = jnp.exp2((scores - top) * EXP2_SCALE).astype(bf16)
        e_ref[p] = e
        for h in range(H):
            heads = slice(D * h, D * (h + 1))
            out = dot(jnp.concatenate([vt[heads, cols], one_rows], axis=0), e[:, 128 * h : 128 * (h + 1)])
            inv = 1.0 / out[D : D + 1]
            inv_ref[p, :, 128 * h : 128 * (h + 1)] = jnp.broadcast_to(inv, (8, 128))
            ot_ref[heads, cols] = out[:D] * inv
    att = transposed(ot_ref[...]).astype(bf16)
    mid = x + dot(att, wout_ref[...])
    t_scr[...] = mid
    mid3 = t_scr[...].reshape(8, 64, E)
    mid_ref[...] = jnp.swapaxes(mid3, 0, 1).reshape(512, E).astype(bf16)


def row_backward(
    zhi_ref, dmid_ref, x_ref, na_ref, qt_ref, kt_ref, va_ref, e_ref, inv_ref, ot_ref, wpad_ref, wout_ref,
    own_ref, other_ref, sums_ref,
    g_scr, dqt_scr, dk_scr, dv_scr,
):
    zhi = zhi_ref[0]
    dmid = jnp.swapaxes(dmid_ref[...].astype(f32).reshape(64, 8, E), 0, 1).reshape(512, E)
    dmid_low = dmid.astype(bf16)
    sum_out = dot(ot_ref[...].astype(bf16), dmid_low)
    d_att = dot_nt(wout_ref[...], dmid_low).astype(bf16).astype(f32)
    zero_rows = jnp.zeros((16, 128), bf16)
    for p in range(4):
        cols = slice(128 * p, 128 * (p + 1))
        blocks = []
        for h in range(H):
            heads = slice(D * h, D * (h + 1))
            d_out = (d_att[heads, cols] * inv_ref[p, 0:1, 128 * h : 128 * (h + 1)]).astype(bf16)
            delta = jnp.sum(d_out.astype(f32) * ot_ref[heads, cols], axis=0, keepdims=True)
            blocks.append(place(d_out, h, split_rows(delta)))
        rhs = jnp.concatenate(blocks, axis=1)
        e = e_ref[p]
        ds = (e.astype(f32) * dot(va_ref[cols, : E + 16], rhs)).astype(bf16)
        for h in range(H):
            heads = slice(D * h, D * (h + 1))
            dqt_scr[heads, cols] = dot(kt_ref[heads, cols], ds[:, 128 * h : 128 * (h + 1)])
        q_rhs = jnp.concatenate(
            [place(qt_ref[D * h : D * (h + 1), cols], h, zero_rows)[:E] for h in range(H)], axis=1
        )
        dk_scr[cols, :] = dot_nt(ds, q_rhs)
        dv_scr[cols, :] = dot_nt(e, rhs[:E])
    dq = pad_lanes((transposed(dqt_scr[...]) * SCALE).astype(bf16))
    dk = pad_lanes((dk_scr[...] * SCALE).astype(bf16))
    dv = pad_lanes(dv_scr[...].astype(bf16))
    na_t = transposed(na_ref[...]).astype(bf16)
    tiles = pack_tiles(dot(na_t, dq), dot(na_t, dk), dot(na_t, dv), pad_lanes(sum_out))
    for t in range(6):
        sums_ref[E * t : E * (t + 1), :] = tiles[t].astype(bf16)
    sums_ref[6 * E :, :] = jnp.zeros((LATE_ROWS - 6 * E, 128), bf16)
    grad = (
        dot_nt(dq, wpad_ref[:, :256]) + dot_nt(dk, wpad_ref[:, 256:512]) + dot_nt(dv, wpad_ref[:, 512:768])
    )
    normed, inv_std = norm(x_ref[...].astype(f32))
    g_scr[...] = dmid + norm_back(normed, inv_std, grad)
    for r in range(8):
        mine = pl.multiple_of(64 * r + 32 * zhi, 32)
        other = pl.multiple_of(64 * r + 32 * (1 - zhi), 32)
        own_ref[32 * r : 32 * (r + 1), :] = g_scr[pl.ds(mine, 32), :].astype(bf16)
        other_ref[32 * r : 32 * (r + 1), :] = g_scr[pl.ds(other, 32), :].astype(bf16)


def hidden_grad(cot_ref, wdown_ref, low_ref, out_ref):
    cot = cot_ref[...].astype(f32).reshape(32, 2, 8, E)
    cot = jnp.concatenate([cot[:, 0], cot[:, 1]], axis=0).reshape(512, E).astype(bf16)
    low_ref[...] = cot
    out_ref[...] = dot_nt(cot, wdown_ref[...])


def column(
    own_ref, sib_ref, bias_ref, cot_ref, dhid_ref, wpad_ref, wt_ref, wout_ref, wup_ref, wdown_ref,
    lay_ref, dmid_ref, nsib_ref, sums_ref,
    ka_scr, va_scr, vt_scr, kt_scr, qt_scr, e_scr, ot_scr, inv_scr, dqt_scr, dk_scr, dv_scr,
):
    n = 512
    mid_own = own_ref[...].astype(f32)
    normed_own, inv_own = norm(mid_own)
    normed_sib, inv_sib = norm(sib_ref[...].astype(f32))
    nb_own = normed_own.astype(bf16)
    nb = jnp.concatenate([nb_own, normed_sib.astype(bf16)], axis=0)
    lane = lax.broadcasted_iota(jnp.int32, (2 * n, 256), 1)
    ka_scr[...] = (dot(nb, wpad_ref[:, 256:512]) + jnp.where(lane == E, bias_ref[...], 0.0)).astype(bf16)
    ones = jnp.where((lane == E) | (lane == E + 1), 1.0, 0.0)
    va_scr[...] = (dot(nb, wpad_ref[:, 512:768]) + ones).astype(bf16)
    qt_scr[...] = dot_nt(wt_ref[:E], nb_own).astype(bf16)
    kt_scr[...] = dot_nt(wt_ref[E : 2 * E], nb).astype(bf16)
    vt_scr[...] = dot_nt(wt_ref[2 * E :], nb).astype(bf16)
    one_rows = jnp.ones((16, 2 * n), bf16)
    at = lax.broadcasted_iota(jnp.int32, (16, n), 0)
    extra = jnp.where(at == 0, 1.0, 0.0).astype(bf16)
    for h in range(H):
        heads = slice(D * h, D * (h + 1))
        scores = dot(ka_scr[:, : E + 16], place(qt_scr[heads, :], h, extra))
        top = jnp.max(scores, axis=0, keepdims=True)
        e = jnp.exp2((scores - top) * EXP2_SCALE).astype(bf16)
        e_scr[h] = e
        out = dot(jnp.concatenate([vt_scr[heads, :], one_rows], axis=0), e)
        inv = 1.0 / out[D : D + 1]
        inv_scr[8 * h : 8 * (h + 1), :] = jnp.broadcast_to(inv, (8, n))
        ot_scr[heads, :] = out[:D] * inv
    att_t = ot_scr[...]
    mid_b = (mid_own + dot(transposed(att_t).astype(bf16), wout_ref[...])).astype(bf16).astype(f32)
    normed_c, inv_c = norm(mid_b)
    nc = normed_c.astype(bf16)
    cot = cot_ref[...]
    pre = dot(nc, wup_ref[...])
    square = pre * pre
    tanh = jnp.tanh(GELU_A * (pre + GELU_B * square * pre))
    half = 0.5 * (1.0 + tanh)
    hidden = (pre * half).astype(bf16)
    slope = half + 0.5 * pre * (1.0 - tanh * tanh) * (GELU_A * (1.0 + 3.0 * GELU_B * square))
    d_pre = (dhid_ref[...] * slope).astype(bf16)
    lay = (mid_b + dot(hidden, wdown_ref[...])).reshape(2, 32, 8, E)
    lay_ref[...] = jnp.stack([lay[0], lay[1]], axis=1).reshape(n, E).astype(bf16)
    cot_t = transposed(cot).astype(bf16)
    nc_t = transposed(normed_c).astype(bf16)
    sum_up = dot(nc_t, d_pre).astype(bf16)
    sum_down = dot(cot_t, hidden).astype(bf16)
    for t in range(6):
        sums_ref[E * (6 + t) : E * (7 + t), :] = sum_up[:, 128 * t : 128 * (t + 1)]
        sums_ref[E * (12 + t) : E * (13 + t), :] = sum_down[:, 128 * t : 128 * (t + 1)]
    d_mid = cot.astype(f32) + norm_back(normed_c, inv_c, dot_nt(d_pre, wup_ref[...]))
    d_mid_low = d_mid.astype(bf16)
    sum_out = dot(att_t.astype(bf16), d_mid_low)
    d_att = dot_nt(wout_ref[...], d_mid_low).astype(bf16).astype(f32)
    zero_rows = jnp.zeros((16, n), bf16)
    for h in range(H):
        heads = slice(D * h, D * (h + 1))
        d_out = (d_att[heads] * inv_scr[8 * h : 8 * h + 1, :]).astype(bf16)
        delta = jnp.sum(d_out.astype(f32) * ot_scr[heads, :], axis=0, keepdims=True)
        rhs = place(d_out, h, split_rows(delta))
        e = e_scr[h]
        ds = (e.astype(f32) * dot(va_scr[:, : E + 16], rhs)).astype(bf16)
        dqt_scr[heads, :] = dot(kt_scr[heads, :], ds)
        dk = dot_nt(ds, place(qt_scr[heads, :], h, zero_rows)[:E])
        dv = dot_nt(e, rhs[:E])
        if h == 0:
            dk_scr[...] = dk
            dv_scr[...] = dv
        else:
            dk_scr[...] += dk
            dv_scr[...] += dv
    dq = pad_lanes((transposed(dqt_scr[...]) * SCALE).astype(bf16))
    dk = pad_lanes((dk_scr[...] * SCALE).astype(bf16))
    dv = pad_lanes(dv_scr[...].astype(bf16))
    nb_t = transposed(nb).astype(bf16)
    tiles = pack_tiles(dot(nb_t[:, :n], dq), dot(nb_t, dk), dot(nb_t, dv), pad_lanes(sum_out))
    for t in range(6):
        sums_ref[E * t : E * (t + 1), :] = tiles[t].astype(bf16)
    sums_ref[18 * E :, :] = jnp.zeros((EARLY_ROWS - 18 * E, 128), bf16)
    grad = dot_nt(dk, wpad_ref[:, 256:512]) + dot_nt(dv, wpad_ref[:, 512:768])
    grad_own = grad[:n] + dot_nt(dq, wpad_ref[:, :256])
    dmid_ref[...] = d_mid_low.astype(f32) + norm_back(normed_own, inv_own, grad_own)
    nsib_ref[...] = norm_back(normed_sib, inv_sib, grad[n:]).astype(bf16)


def sum_shares(in_ref, out_ref):
    total = jnp.sum(in_ref[...].astype(f32), axis=0).astype(bf16)
    out_ref[...] = jnp.broadcast_to(total[None], out_ref.shape)


def finish_early(sums_ref, qkv_ref, out_ref, up_ref, down_ref):
    factor = 2.0 ** -8
    tile = lambda t: sums_ref[E * t : E * (t + 1), :].astype(f32)
    unpack_tiles(tile, qkv_ref, out_ref, factor)
    for t in range(6):
        up_ref[:, 128 * t : 128 * (t + 1)] = tile(6 + t) * factor
        down_ref[128 * t : 128 * (t + 1), :] = jnp.transpose(tile(12 + t) * factor)


def finish_late(sums_ref, qkv_ref, out_ref):
    tile = lambda t: sums_ref[E * t : E * (t + 1), :].astype(f32)
    unpack_tiles(tile, qkv_ref, out_ref, 2.0 ** -8)


def call(kernel, outs, scratch=(), flops=0, smem=0, name=None):
    vmem = pl.BlockSpec(memory_space=pltpu.VMEM)

    def run(*args):
        in_specs = [pl.BlockSpec(memory_space=pltpu.SMEM)] * smem + [vmem] * (len(args) - smem)
        moved = sum(a.size * a.dtype.itemsize for a in args)
        return pl.pallas_call(
            kernel,
            out_shape=[jax.ShapeDtypeStruct(s, t) for s, t in outs],
            in_specs=in_specs,
            out_specs=[vmem] * len(outs),
            scratch_shapes=[pltpu.VMEM(s, t) for s, t in scratch],
            compiler_params=pltpu.CompilerParams(vmem_limit_bytes=48 * 1024 * 1024),
            cost_estimate=pl.CostEstimate(flops=flops, bytes_accessed=moved, transcendentals=0),
            name=name,
        )(*args)

    return run


def shards(cells, split, w_qkv_feat, w_out_feat, w_qkv_samp, w_out_samp, w_up, w_down, cotangent):
    zhi = lax.axis_index("zhi")
    core = lax.axis_index("core")
    group = ("zhi", "chip")
    everyone = ("chip", "core", "zhi")
    pad = lambda w: jnp.pad(w.reshape(E, 3, E), ((0, 0), (0, 0), (0, 64))).reshape(E, 768)
    wf_pad, ws_pad = pad(w_qkv_feat), pad(w_qkv_samp)
    wf_t, ws_t = w_qkv_feat.T, w_qkv_samp.T
    zhi_arr = zhi.astype(jnp.int32).reshape(1)

    sent = lax.dynamic_slice_in_dim(cells, 8 * (1 - zhi), 8, 0).reshape(256, E)
    recv = lax.ppermute(sent, "zhi", [(0, 1), (1, 0)])
    cot_sent = cotangent.transpose(1, 0, 2)
    cot_recv = lax.all_to_all(cot_sent, "chip", 0, 0, tiled=True).reshape(512, E)

    mid, x, na, qt, kt, va, e, inv, ot = call(
        row_forward,
        [
            ((512, E), bf16), ((512, E), bf16), ((512, E), bf16), ((E, 512), bf16), ((E, 512), bf16),
            ((512, 256), bf16), ((4, 128, 768), bf16), ((4, 8, 768), f32), ((E, 512), f32),
        ],
        [((512, E), f32), ((512, E), f32)],
        flops=600_000_000, smem=1, name="row_forward",
    )(zhi_arr, cells.reshape(512, E), recv, wf_pad, wf_t, w_out_feat)

    mid_own = lax.all_to_all(mid.reshape(64, 8, E), group, 0, 0, tiled=True).reshape(512, E)
    mid_sib = lax.ppermute(mid_own, "core", [(0, 1), (1, 0)])

    cot, d_hidden = call(
        hidden_grad, [((512, E), bf16), ((512, 768), f32)], flops=150_000_000, name="hidden_grad"
    )(cot_recv, w_down)
    train = jnp.arange(16, dtype=jnp.int32)[None, :] < split[:, None]
    bias = jnp.where(train, 0.0, NEG).astype(f32).reshape(32, 2, 2, 8).transpose(1, 2, 0, 3).reshape(2, 512)
    bias = jnp.where(core == 0, bias, bias[::-1]).reshape(1024, 1)

    lay, d_own, n_sib, early = call(
        column,
        [((512, E), bf16), ((512, E), f32), ((512, E), bf16), ((EARLY_ROWS, 128), bf16)],
        [
            ((1024, 256), bf16), ((1024, 256), bf16), ((E, 1024), bf16), ((E, 1024), bf16), ((E, 512), bf16),
            ((H, 1024, 512), bf16), ((E, 512), f32), ((8 * H, 512), f32), ((E, 512), f32),
            ((1024, E), f32), ((1024, E), f32),
        ],
        flops=8_000_000_000, name="column",
    )(mid_own, mid_sib, bias, cot, d_hidden, ws_pad, ws_t, w_out_samp, w_up, w_down)

    n_recv = lax.ppermute(n_sib, "core", [(0, 1), (1, 0)])
    d_mid = (d_own + n_recv.astype(f32)).astype(bf16)
    d_mid_rows = lax.all_to_all(d_mid.reshape(64, 8, E), group, 0, 0, tiled=True).reshape(512, E)

    lay_recv = lax.all_to_all(lay.reshape(32, 16, E), "chip", 0, 0, tiled=True)
    layer_out = lay_recv.transpose(1, 0, 2)
    early_recv = lax.all_to_all(early.reshape(128, EARLY_ROWS // 128, 128), everyone, 0, 0, tiled=True)

    own, other, late = call(
        row_backward,
        [((256, E), bf16), ((256, E), bf16), ((LATE_ROWS, 128), bf16)],
        [((512, E), f32), ((E, 512), f32), ((512, E), f32), ((512, E), f32)],
        flops=1_500_000_000, smem=1, name="row_backward",
    )(zhi_arr, d_mid_rows, x, na, qt, kt, va, e, inv, ot, wf_pad, w_out_feat)

    late_recv = lax.all_to_all(late.reshape(128, LATE_ROWS // 128, 128), everyone, 0, 0, tiled=True)
    back = lax.ppermute(other, "zhi", [(0, 1), (1, 0)])
    grad_cells = jnp.where(
        zhi == 0, jnp.concatenate([own, back], axis=0), jnp.concatenate([back, own], axis=0)
    ).reshape(16, 32, E)

    (early_out,) = call(sum_shares, [((128, EARLY_ROWS // 128, 128), bf16)], flops=10_000_000, name="sum_early")(early_recv)
    early_all = lax.all_to_all(early_out, everyone, 0, 0, tiled=True).reshape(EARLY_ROWS, 128)
    (late_out,) = call(sum_shares, [((128, LATE_ROWS // 128, 128), bf16)], flops=10_000_000, name="sum_late")(late_recv)
    late_all = lax.all_to_all(late_out, everyone, 0, 0, tiled=True).reshape(LATE_ROWS, 128)
    g_qkv_samp, g_out_samp, g_up, g_down = call(
        finish_early, [((E, 576), f32), ((E, E), f32), ((E, 768), f32), ((768, E), f32)], flops=10_000_000, name="finish_early"
    )(early_all)
    g_qkv_feat, g_out_feat = call(finish_late, [((E, 576), f32), ((E, E), f32)], flops=10_000_000, name="finish_late")(late_all)
    return layer_out, grad_cells, g_qkv_feat, g_out_feat, g_qkv_samp, g_out_samp, g_up, g_down


def solution(mesh):
    wide = Mesh(mesh.devices.reshape(32, 2, 2), ("chip", "core", "zhi"))
    cells = P(("chip", "core"), "zhi", None)
    return jax.shard_map(
        shards,
        mesh=wide,
        in_specs=(cells, P(), P(), P(), P(), P(), P(), P(), cells),
        out_specs=(cells, cells, P(), P(), P(), P(), P(), P()),
        check_vma=False,
    )
```

```python
import jax
import jax.numpy as jnp
from jax import lax
from jax.experimental import pallas as pl
from jax.experimental.pallas import tpu as pltpu
from jax.sharding import Mesh, PartitionSpec as P

H = 6
D = 32
E = 192
EPS = 1e-05
SCALE = D ** -0.5
EXP2_SCALE = SCALE * 1.4426950408889634
NEG = -1e30
GELU_A = 0.7978845608028654
GELU_B = 0.044715
f32 = jnp.float32
bf16 = jnp.bfloat16
EARLY = 9 * E
LATE = 3 * E
CHUNK = 40
SHARE = 64 * CHUNK


def dot(a, b):
    return jnp.dot(a, b, preferred_element_type=f32)


def dot_nt(a, b):
    return lax.dot_general(a, b, (((1,), (1,)), ((), ())), preferred_element_type=f32)


def transposed(v):
    return jnp.transpose(v.astype(f32))


def norm(v):
    centered = v - jnp.mean(v, axis=-1, keepdims=True)
    inv_std = lax.rsqrt(jnp.mean(centered * centered, axis=-1, keepdims=True) + EPS)
    return centered * inv_std, inv_std


def norm_back(normed, inv_std, grad):
    return inv_std * (
        grad
        - jnp.mean(grad, axis=-1, keepdims=True)
        - normed * jnp.mean(grad * normed, axis=-1, keepdims=True)
    )


def place(rows, head, extra):
    count = rows.shape[1]
    parts = []
    if head > 0:
        parts.append(jnp.zeros((D * head, count), bf16))
    parts.append(rows)
    if head < H - 1:
        parts.append(jnp.zeros((E - D * (head + 1), count), bf16))
    parts.append(extra)
    return jnp.concatenate(parts, axis=0)


def split_rows(delta):
    high = (-delta).astype(bf16).astype(f32)
    low = -delta - high
    at = lax.broadcasted_iota(jnp.int32, (16, delta.shape[1]), 0)
    return jnp.where(at == 0, high, jnp.where(at == 1, low, 0.0)).astype(bf16)


def pack_tiles(q, k, v, out):
    lane = lax.broadcasted_iota(jnp.int32, (E, 128), 1)
    roll = lambda t: pltpu.roll(t, 64, 1)
    low = lane < 64
    return (
        q[:, :128],
        jnp.where(low, q[:, 128:], roll(k[:, :128])),
        jnp.where(low, roll(k[:, :128]), roll(k[:, 128:])),
        v[:, :128],
        out[:, :128],
        jnp.where(low, v[:, 128:], roll(out[:, 128:])),
    )


def unpack_tiles(tile, qkv_ref, out_ref, factor):
    for t in range(4):
        qkv_ref[:, 128 * t : 128 * (t + 1)] = tile(t) * factor
    last = tile(5) * factor
    qkv_ref[:, 512:576] = last[:, :64]
    out_ref[:, :128] = tile(4) * factor
    out_ref[:, 128:192] = pltpu.roll(last, 64, 1)[:, :64]


def pad_lanes(v):
    return jnp.concatenate([v, jnp.zeros((v.shape[0], 256 - E), v.dtype)], axis=1)


def halve(core_ref, sums_scr, keep_ref, send_ref, rows):
    core = core_ref[0]
    keep_ref[...] = sums_scr[pl.ds(pl.multiple_of(core * rows, 64), rows), :]
    send_ref[...] = sums_scr[pl.ds(pl.multiple_of((1 - core) * rows, 64), rows), :]


def row_forward(
    zhi_ref, cells_ref, cot_ref, recv_ref, wpad_ref, wt_ref, wout_ref,
    mid_ref, *rest,
):
    saved, (x_scr, x_ref, qk_ref, va_ref, e_ref, inv_ref, ot_ref, sems) = rest[:6], rest[6:]
    copies = [
        pltpu.make_async_copy(scr, out, sems.at[i])
        for i, (scr, out) in enumerate(zip((x_ref, qk_ref, va_ref, e_ref, inv_ref, ot_ref), saved))
    ]
    zhi = zhi_ref[0]
    for r in range(8):
        mine = pl.multiple_of(64 * r + 32 * zhi, 32)
        other = pl.multiple_of(64 * r + 32 * (1 - zhi), 32)
        src = pl.multiple_of(256 * zhi + 32 * r, 32)
        own = (cells_ref[pl.ds(src, 32), :].astype(f32), cot_ref[pl.ds(src, 32), :].astype(f32))
        x_scr[pl.ds(mine, 32), :] = jnp.concatenate(own, axis=1)
        x_scr[pl.ds(other, 32), :] = recv_ref[32 * r : 32 * (r + 1), :].astype(f32)
    x = x_scr[:, :E]
    x_ref[...] = x.astype(bf16)
    copies[0].start()
    normed, _ = norm(x)
    na = normed.astype(bf16)
    qkv_t = dot_nt(wt_ref[...], na).astype(bf16)
    qk_ref[...] = qkv_t[: 2 * E]
    copies[1].start()
    vt = qkv_t[2 * E :]
    lane = lax.broadcasted_iota(jnp.int32, (512, 256), 1)
    row = lax.broadcasted_iota(jnp.int32, (512, 256), 0)
    odd = (row // 64) % 2
    flags = jnp.where((lane == E) & (odd == 0), 1.0, jnp.where((lane == E + 1) & (odd == 1), 1.0, 0.0))
    ka = (dot(na, wpad_ref[:, 256:512]) + flags).astype(bf16)
    ones = jnp.where((lane == E) | (lane == E + 1), 1.0, 0.0)
    va_ref[...] = (dot(na, wpad_ref[:, 512:768]) + ones).astype(bf16)
    copies[2].start()
    at = lax.broadcasted_iota(jnp.int32, (16, 128), 0)
    col = lax.broadcasted_iota(jnp.int32, (16, 128), 1)
    other_row = ((at == 0) & (col >= 64)) | ((at == 1) & (col < 64))
    extra = jnp.where(other_row, NEG, 0.0).astype(bf16)
    one_rows = jnp.ones((16, 128), bf16)
    for p in range(4):
        cols = slice(128 * p, 128 * (p + 1))
        rhs = jnp.concatenate(
            [place(qkv_t[D * h : D * (h + 1), cols], h, extra) for h in range(H)], axis=1
        )
        scores = dot(ka[cols, : E + 16], rhs)
        top = jnp.max(scores, axis=0, keepdims=True)
        e = jnp.exp2((scores - top) * EXP2_SCALE).astype(bf16)
        e_ref[p] = e
        for h in range(H):
            heads = slice(D * h, D * (h + 1))
            out = dot(jnp.concatenate([vt[heads, cols], one_rows], axis=0), e[:, 128 * h : 128 * (h + 1)])
            inv = 1.0 / out[D : D + 1]
            inv_ref[p, :, 128 * h : 128 * (h + 1)] = jnp.broadcast_to(inv, (8, 128))
            ot_ref[heads, cols] = out[:D] * inv
    for copy in copies[3:]:
        copy.start()
    att = transposed(ot_ref[...]).astype(bf16)
    mid = x + dot(att, wout_ref[...])
    both = jnp.concatenate([mid, x_scr[:, E:]], axis=1).reshape(8, 64, 2 * E)
    mid_ref[...] = jnp.swapaxes(both, 0, 1).reshape(512, 2 * E).astype(bf16)
    for copy in copies:
        copy.wait()


def row_backward(
    zhi_ref, core_ref, dmid_ref, wpad_ref, wout_ref, *rest,
):
    saved, rest = rest[:6], rest[6:]
    own_ref, other_ref, keep_ref, send_ref, sums_scr, g_scr, dqt_scr, dk_scr, dv_scr = rest[:9]
    x_ref, qk_ref, va_ref, e_ref, inv_ref, ot_ref, sems = rest[9:]
    copies = [
        pltpu.make_async_copy(src, scr, sems.at[i])
        for i, (src, scr) in enumerate(zip(saved, (x_ref, qk_ref, va_ref, e_ref, inv_ref, ot_ref)))
    ]
    for copy in copies:
        copy.start()
    zhi = zhi_ref[0]
    both = jnp.swapaxes(dmid_ref[...].astype(f32).reshape(64, 8, 2 * E), 0, 1).reshape(512, 2 * E)
    dmid = both[:, :E]
    dmid_low = dmid.astype(bf16)
    for copy in copies:
        copy.wait()
    sum_out = dot(ot_ref[...].astype(bf16), dmid_low)
    d_att = dot_nt(wout_ref[...], dmid_low).astype(bf16).astype(f32)
    zero_rows = jnp.zeros((16, 128), bf16)
    for p in range(4):
        cols = slice(128 * p, 128 * (p + 1))
        blocks = []
        for h in range(H):
            heads = slice(D * h, D * (h + 1))
            d_out = (d_att[heads, cols] * inv_ref[p, 0:1, 128 * h : 128 * (h + 1)]).astype(bf16)
            delta = jnp.sum(d_out.astype(f32) * ot_ref[heads, cols], axis=0, keepdims=True)
            blocks.append(place(d_out, h, split_rows(delta)))
        rhs = jnp.concatenate(blocks, axis=1)
        e = e_ref[p]
        ds = (e.astype(f32) * dot(va_ref[cols, : E + 16], rhs)).astype(bf16)
        for h in range(H):
            heads = slice(D * h, D * (h + 1))
            dqt_scr[heads, cols] = dot(qk_ref[E + D * h : E + D * (h + 1), cols], ds[:, 128 * h : 128 * (h + 1)])
        q_rhs = jnp.concatenate(
            [place(qk_ref[D * h : D * (h + 1), cols], h, zero_rows)[:E] for h in range(H)], axis=1
        )
        dk_scr[cols, :] = dot_nt(ds, q_rhs)
        dv_scr[cols, :] = dot_nt(e, rhs[:E])
    dq = pad_lanes((transposed(dqt_scr[...]) * SCALE).astype(bf16))
    dk = pad_lanes((dk_scr[...] * SCALE).astype(bf16))
    dv = pad_lanes(dv_scr[...].astype(bf16))
    normed, inv_std = norm(x_ref[...].astype(f32))
    na_t = transposed(normed.astype(bf16)).astype(bf16)
    tiles = pack_tiles(dot(na_t, dq), dot(na_t, dk), dot(na_t, dv), pad_lanes(sum_out))
    for t in range(6):
        sums_scr[E * t : E * (t + 1), :] = tiles[t].astype(bf16)
    halve(core_ref, sums_scr, keep_ref, send_ref, LATE)
    grad = (
        dot_nt(dq, wpad_ref[:, :256]) + dot_nt(dk, wpad_ref[:, 256:512]) + dot_nt(dv, wpad_ref[:, 512:768])
    )
    g_scr[...] = jnp.concatenate([dmid + norm_back(normed, inv_std, grad), both[:, E:]], axis=1)
    for r in range(8):
        mine = pl.multiple_of(64 * r + 32 * zhi, 32)
        other = pl.multiple_of(64 * r + 32 * (1 - zhi), 32)
        own_ref[32 * r : 32 * (r + 1), :] = g_scr[pl.ds(mine, 32), :].astype(bf16)
        other_ref[32 * r : 32 * (r + 1), :] = g_scr[pl.ds(other, 32), :].astype(bf16)


def column(
    core_ref, own_ref, sib_ref, bias_ref, wpad_ref, wt_ref, wout_ref, wup_ref, wdown_ref,
    lay_ref, dmid_ref, nsib_ref, keep_ref, send_ref,
    sums_scr, ka_scr, va_scr, vt_scr, kt_scr, qt_scr, e_scr, ot_scr, inv_scr, dqt_scr, dk_scr, dv_scr,
):
    n = 512
    mid_own = own_ref[:, :E].astype(f32)
    normed_own, inv_own = norm(mid_own)
    normed_sib, inv_sib = norm(sib_ref[:, :E].astype(f32))
    nb_own = normed_own.astype(bf16)
    nb = jnp.concatenate([nb_own, normed_sib.astype(bf16)], axis=0)
    lane = lax.broadcasted_iota(jnp.int32, (2 * n, 256), 1)
    ka_scr[...] = (dot(nb, wpad_ref[:, 256:512]) + jnp.where(lane == E, bias_ref[...], 0.0)).astype(bf16)
    ones = jnp.where((lane == E) | (lane == E + 1), 1.0, 0.0)
    va_scr[...] = (dot(nb, wpad_ref[:, 512:768]) + ones).astype(bf16)
    qt_scr[...] = dot_nt(wt_ref[:E], nb_own).astype(bf16)
    kt_scr[...] = dot_nt(wt_ref[E : 2 * E], nb).astype(bf16)
    vt_scr[...] = dot_nt(wt_ref[2 * E :], nb).astype(bf16)
    one_rows = jnp.ones((16, 2 * n), bf16)
    at = lax.broadcasted_iota(jnp.int32, (16, n), 0)
    extra = jnp.where(at == 0, 1.0, 0.0).astype(bf16)
    for h in range(H):
        heads = slice(D * h, D * (h + 1))
        scores = dot(ka_scr[:, : E + 16], place(qt_scr[heads, :], h, extra))
        top = jnp.max(scores, axis=0, keepdims=True)
        e = jnp.exp2((scores - top) * EXP2_SCALE).astype(bf16)
        e_scr[h] = e
        out = dot(jnp.concatenate([vt_scr[heads, :], one_rows], axis=0), e)
        inv = 1.0 / out[D : D + 1]
        inv_scr[8 * h : 8 * (h + 1), :] = jnp.broadcast_to(inv, (8, n))
        ot_scr[heads, :] = out[:D] * inv
    att_t = ot_scr[...]
    mid_b = (mid_own + dot(transposed(att_t).astype(bf16), wout_ref[...])).astype(bf16).astype(f32)
    normed_c, inv_c = norm(mid_b)
    nc = normed_c.astype(bf16)
    cot = own_ref[:, E:]
    pre = dot(nc, wup_ref[...])
    square = pre * pre
    tanh = jnp.tanh(GELU_A * (pre + GELU_B * square * pre))
    half = 0.5 * (1.0 + tanh)
    hidden = (pre * half).astype(bf16)
    slope = half + 0.5 * pre * (1.0 - tanh * tanh) * (GELU_A * (1.0 + 3.0 * GELU_B * square))
    d_pre = (dot(cot, wdown_ref[...]) * slope).astype(bf16)
    lay_ref[...] = mid_b + dot_nt(hidden, wdown_ref[...])
    cot_t = transposed(cot).astype(bf16)
    nc_t = transposed(normed_c).astype(bf16)
    sum_up = dot(nc_t, d_pre).astype(bf16)
    sum_down = dot(cot_t, hidden).astype(bf16)
    for t in range(6):
        sums_scr[E * (6 + t) : E * (7 + t), :] = sum_up[:, 128 * t : 128 * (t + 1)]
        sums_scr[E * (12 + t) : E * (13 + t), :] = sum_down[:, 128 * t : 128 * (t + 1)]
    d_mid = cot.astype(f32) + norm_back(normed_c, inv_c, dot_nt(d_pre, wup_ref[...]))
    d_mid_low = d_mid.astype(bf16)
    sum_out = dot(att_t.astype(bf16), d_mid_low)
    d_att = dot_nt(wout_ref[...], d_mid_low).astype(bf16).astype(f32)
    zero_rows = jnp.zeros((16, n), bf16)
    for h in range(H):
        heads = slice(D * h, D * (h + 1))
        d_out = (d_att[heads] * inv_scr[8 * h : 8 * h + 1, :]).astype(bf16)
        delta = jnp.sum(d_out.astype(f32) * ot_scr[heads, :], axis=0, keepdims=True)
        rhs = place(d_out, h, split_rows(delta))
        e = e_scr[h]
        ds = (e.astype(f32) * dot(va_scr[:, : E + 16], rhs)).astype(bf16)
        dqt_scr[heads, :] = dot(kt_scr[heads, :], ds)
        dk = dot_nt(ds, place(qt_scr[heads, :], h, zero_rows)[:E])
        dv = dot_nt(e, rhs[:E])
        if h == 0:
            dk_scr[...] = dk
            dv_scr[...] = dv
        else:
            dk_scr[...] += dk
            dv_scr[...] += dv
    dq = pad_lanes((transposed(dqt_scr[...]) * SCALE).astype(bf16))
    dk = pad_lanes((dk_scr[...] * SCALE).astype(bf16))
    dv = pad_lanes(dv_scr[...].astype(bf16))
    nb_t = transposed(nb).astype(bf16)
    tiles = pack_tiles(dot(nb_t[:, :n], dq), dot(nb_t, dk), dot(nb_t, dv), pad_lanes(sum_out))
    for t in range(6):
        sums_scr[E * t : E * (t + 1), :] = tiles[t].astype(bf16)
    halve(core_ref, sums_scr, keep_ref, send_ref, EARLY)
    grad = dot_nt(dk, wpad_ref[:, 256:512]) + dot_nt(dv, wpad_ref[:, 512:768])
    grad_own = grad[:n] + dot_nt(dq, wpad_ref[:, :256])
    dmid_ref[...] = d_mid_low.astype(f32) + norm_back(normed_own, inv_own, grad_own)
    nsib_ref[...] = norm_back(normed_sib, inv_sib, grad[n:]).astype(bf16)


def sum_shares(zhi_ref, parts_ref, own_ref, back_ref, out_ref, grad_ref, lay_ref):
    total = jnp.sum(parts_ref[...].astype(f32), axis=0).astype(bf16)
    out_ref[...] = jnp.broadcast_to(total[None], out_ref.shape)
    zhi = zhi_ref[0]
    for ref, at in ((own_ref, zhi), (back_ref, 1 - zhi)):
        rows = pl.ds(pl.multiple_of(256 * at, 256), 256)
        grad_ref[rows, :] = ref[:, :E]
        lay_ref[rows, :] = ref[:, E:]


def join(d_own_ref, n_recv_ref, lay_ref, out_ref):
    d_mid = d_own_ref[...] + n_recv_ref[...].astype(f32)
    out_ref[...] = jnp.concatenate([d_mid, lay_ref[...]], axis=1).astype(bf16)


def merge(early_keep_ref, early_recv_ref, late_keep_ref, late_recv_ref, out_ref):
    out_ref[:EARLY, :] = (early_keep_ref[...].astype(f32) + early_recv_ref[...].astype(f32)).astype(bf16)
    out_ref[EARLY : EARLY + LATE, :] = (late_keep_ref[...].astype(f32) + late_recv_ref[...].astype(f32)).astype(bf16)
    out_ref[EARLY + LATE :, :] = jnp.zeros((SHARE - EARLY - LATE, 128), bf16)


def finish(core_ref, own_ref, sib_ref, qkv_f_ref, out_f_ref, qkv_s_ref, out_s_ref, up_ref, down_ref, scr):
    core = core_ref[0]
    rows = EARLY + LATE
    scr[pl.ds(pl.multiple_of(core * rows, 64), rows), :] = own_ref[:rows, :]
    scr[pl.ds(pl.multiple_of((1 - core) * rows, 64), rows), :] = sib_ref[:rows, :]
    factor = 2.0 ** -8

    def early(t):
        at = E * t if t < 9 else E * t + LATE
        return scr[at : at + E, :].astype(f32)

    def late(t):
        at = EARLY + E * t if t < 3 else 2 * EARLY + E * t
        return scr[at : at + E, :].astype(f32)

    unpack_tiles(early, qkv_s_ref, out_s_ref, factor)
    unpack_tiles(late, qkv_f_ref, out_f_ref, factor)
    for t in range(6):
        up_ref[:, 128 * t : 128 * (t + 1)] = early(6 + t) * factor
        down_ref[:, 128 * t : 128 * (t + 1)] = early(12 + t) * factor


def call(kernel, outs, scratch=(), flops=0, smem=0, name=None, mib=12, in_hbm=0, out_hbm=0, sems=0):
    vmem = pl.BlockSpec(memory_space=pltpu.VMEM)
    hbm = pl.BlockSpec(memory_space=pltpu.HBM)

    def run(*args):
        in_specs = [pl.BlockSpec(memory_space=pltpu.SMEM)] * smem + [vmem] * (len(args) - smem - in_hbm) + [hbm] * in_hbm
        moved = sum(a.size * a.dtype.itemsize for a in args)
        return pl.pallas_call(
            kernel,
            out_shape=[jax.ShapeDtypeStruct(s, t) for s, t in outs],
            in_specs=in_specs,
            out_specs=[vmem] * (len(outs) - out_hbm) + [hbm] * out_hbm,
            scratch_shapes=[pltpu.VMEM(s, t) for s, t in scratch] + [pltpu.SemaphoreType.DMA((sems,))] * (sems > 0),
            compiler_params=pltpu.CompilerParams(vmem_limit_bytes=mib * 1024 * 1024),
            cost_estimate=pl.CostEstimate(flops=flops, bytes_accessed=moved, transcendentals=0),
            name=name,
        )(*args)

    return run


def shards(cells, split, w_qkv_feat, w_out_feat, w_qkv_samp, w_out_samp, w_up, w_down, cotangent):
    zhi = lax.axis_index("zhi")
    core = lax.axis_index("core")
    group = ("zhi", "chip")
    swap = [(0, 1), (1, 0)]
    pad = lambda w: jnp.pad(w.reshape(E, 3, E), ((0, 0), (0, 0), (0, 64))).reshape(E, 768)
    wf_pad, ws_pad = pad(w_qkv_feat), pad(w_qkv_samp)
    wf_t, ws_t = w_qkv_feat.T, w_qkv_samp.T
    zhi_arr = zhi.astype(jnp.int32).reshape(1)
    core_arr = core.astype(jnp.int32).reshape(1)

    take = lambda v: lax.dynamic_slice_in_dim(v, 8 * (1 - zhi), 8, 0).reshape(256, E)
    sent = jnp.concatenate([take(cells), take(cotangent)], axis=1)
    recv = lax.ppermute(sent, "zhi", swap)

    kept = [
        ((512, E), bf16), ((2 * E, 512), bf16), ((512, 256), bf16),
        ((4, 128, 768), bf16), ((4, 8, 768), f32), ((E, 512), f32),
    ]
    mid, *saved = call(
        row_forward,
        [((512, 2 * E), bf16)] + kept,
        [((512, 2 * E), f32)] + kept,
        flops=600_000_000, smem=1, name="row_forward", out_hbm=6, sems=6,
    )(zhi_arr, cells.reshape(512, E), cotangent.reshape(512, E), recv, wf_pad, wf_t, w_out_feat)

    train = jnp.arange(16, dtype=jnp.int32)[None, :] < split[:, None]
    bias = jnp.where(train, 0.0, NEG).astype(f32).reshape(32, 2, 2, 8).transpose(1, 2, 0, 3).reshape(2, 512)
    bias = jnp.where(core == 0, bias, bias[::-1]).reshape(1024, 1)
    mid, bias, ws_pad, ws_t = lax.optimization_barrier((mid, bias, ws_pad, ws_t))
    own = lax.all_to_all(mid.reshape(64, 8, 2 * E), group, 0, 0, tiled=True).reshape(512, 2 * E)
    sib = lax.ppermute(own, "core", swap)

    lay, d_own, n_sib, early_keep, early_send = call(
        column,
        [((512, E), f32), ((512, E), f32), ((512, E), bf16), ((EARLY, 128), bf16), ((EARLY, 128), bf16)],
        [
            ((2 * EARLY, 128), bf16),
            ((1024, 256), bf16), ((1024, 256), bf16), ((E, 1024), bf16), ((E, 1024), bf16), ((E, 512), bf16),
            ((H, 1024, 512), bf16), ((E, 512), f32), ((8 * H, 512), f32), ((E, 512), f32),
            ((1024, E), f32), ((1024, E), f32),
        ],
        flops=8_000_000_000, smem=1, name="column", mib=32,
    )(core_arr, own, sib, bias, ws_pad, ws_t, w_out_samp, w_up, w_down.T)

    n_recv = lax.ppermute(n_sib, "core", swap)
    early_recv = lax.ppermute(early_send, "core", swap)
    (joined,) = call(join, [((512, 2 * E), bf16)], flops=10_000_000, name="join")(d_own, n_recv, lay)
    rows = lax.all_to_all(joined.reshape(64, 8, 2 * E), group, 0, 0, tiled=True).reshape(512, 2 * E)

    mine, other, late_keep, late_send = call(
        row_backward,
        [((256, 2 * E), bf16), ((256, 2 * E), bf16), ((LATE, 128), bf16), ((LATE, 128), bf16)],
        [((2 * LATE, 128), bf16), ((512, 2 * E), f32), ((E, 512), f32), ((512, E), f32), ((512, E), f32)] + kept,
        flops=1_500_000_000, smem=2, name="row_backward", in_hbm=6, sems=6,
    )(zhi_arr, core_arr, rows, wf_pad, w_out_feat, *saved)

    late_recv = lax.ppermute(late_send, "core", swap)
    (share,) = call(merge, [((SHARE, 128), bf16)], flops=10_000_000, name="merge")(
        early_keep, early_recv, late_keep, late_recv
    )
    parts = lax.all_to_all(share.reshape(64, CHUNK, 128), group, 0, 0, tiled=True)
    back = lax.ppermute(other, "zhi", swap)
    total, grad_cells, layer_out = call(
        sum_shares,
        [((64, CHUNK, 128), bf16), ((512, E), bf16), ((512, E), bf16)],
        flops=10_000_000, smem=1, name="sum_shares",
    )(zhi_arr, parts, mine, back)
    sums = lax.all_to_all(total, group, 0, 0, tiled=True).reshape(SHARE, 128)
    sums_sib = lax.ppermute(sums, "core", swap)
    g_qkv_feat, g_out_feat, g_qkv_samp, g_out_samp, g_up, g_down_t = call(
        finish,
        [((E, 576), f32), ((E, E), f32), ((E, 576), f32), ((E, E), f32), ((E, 768), f32), ((E, 768), f32)],
        [((2 * (EARLY + LATE), 128), bf16)],
        flops=10_000_000, smem=1, name="finish",
    )(core_arr, sums, sums_sib)
    return (
        layer_out.reshape(16, 32, E), grad_cells.reshape(16, 32, E),
        g_qkv_feat, g_out_feat, g_qkv_samp, g_out_samp, g_up, g_down_t.T,
    )


def solution(mesh):
    wide = Mesh(mesh.devices.reshape(32, 2, 2), ("chip", "core", "zhi"))
    cells = P(("chip", "core"), "zhi", None)
    return jax.shard_map(
        shards,
        mesh=wide,
        in_specs=(cells, P(), P(), P(), P(), P(), P(), P(), cells),
        out_specs=(cells, cells, P(), P(), P(), P(), P(), P()),
        check_vma=False,
    )
```

```python
import jax
import jax.numpy as jnp
from jax import lax
from jax.experimental import pallas as pl
from jax.experimental.pallas import tpu as pltpu
from jax.sharding import Mesh, PartitionSpec as P

H = 6
D = 32
E = 192
EPS = 1e-05
SCALE = D ** -0.5
EXP2_SCALE = SCALE * 1.4426950408889634
NEG = -1e30
GELU_A = 0.7978845608028654
GELU_B = 0.044715
f32 = jnp.float32
bf16 = jnp.bfloat16
EARLY = 9 * E
LATE = 3 * E
CHUNK = 40
SHARE = 64 * CHUNK


def dot(a, b):
    return jnp.dot(a, b, preferred_element_type=f32)


def dot_nt(a, b):
    return lax.dot_general(a, b, (((1,), (1,)), ((), ())), preferred_element_type=f32)


def transposed(v):
    return jnp.transpose(v.astype(f32))


def lane_mean(v):
    return dot(v.astype(bf16), jnp.full((E, E), 1.0, bf16)) * (1.0 / E)


def norm(v):
    centered = v - lane_mean(v)
    inv_std = lax.rsqrt(lane_mean(centered * centered) + EPS)
    return centered * inv_std, inv_std


def norm_back(normed, inv_std, grad):
    return inv_std * (grad - lane_mean(grad) - normed * lane_mean(grad * normed))


def place(rows, head, extra):
    count = rows.shape[1]
    parts = []
    if head > 0:
        parts.append(jnp.zeros((D * head, count), bf16))
    parts.append(rows)
    if head < H - 1:
        parts.append(jnp.zeros((E - D * (head + 1), count), bf16))
    parts.append(extra)
    return jnp.concatenate(parts, axis=0)


def split_rows(delta):
    high = (-delta).astype(bf16).astype(f32)
    low = -delta - high
    at = lax.broadcasted_iota(jnp.int32, (16, delta.shape[1]), 0)
    return jnp.where(at == 0, high, jnp.where(at == 1, low, 0.0)).astype(bf16)


def pack_tiles(q, k, v, out):
    lane = lax.broadcasted_iota(jnp.int32, (E, 128), 1)
    roll = lambda t: pltpu.roll(t, 64, 1)
    low = lane < 64
    return (
        q[:, :128],
        jnp.where(low, q[:, 128:], roll(k[:, :128])),
        jnp.where(low, roll(k[:, :128]), roll(k[:, 128:])),
        v[:, :128],
        out[:, :128],
        jnp.where(low, v[:, 128:], roll(out[:, 128:])),
    )


def unpack_tiles(tile, qkv_ref, out_ref, factor):
    for t in range(4):
        qkv_ref[:, 128 * t : 128 * (t + 1)] = tile(t) * factor
    last = tile(5) * factor
    qkv_ref[:, 512:576] = last[:, :64]
    out_ref[:, :128] = tile(4) * factor
    out_ref[:, 128:192] = pltpu.roll(last, 64, 1)[:, :64]


def pad_lanes(v):
    return jnp.concatenate([v, jnp.zeros((v.shape[0], 256 - E), v.dtype)], axis=1)


def halve(core_ref, sums_scr, keep_ref, send_ref, rows):
    core = core_ref[0]
    keep_ref[...] = sums_scr[pl.ds(pl.multiple_of(core * rows, 64), rows), :]
    send_ref[...] = sums_scr[pl.ds(pl.multiple_of((1 - core) * rows, 64), rows), :]


def attend(x, wt_ref, ot_ref, keep=None):
    na = norm(x)[0].astype(bf16)
    qkv_t = dot_nt(wt_ref[...], na).astype(bf16)
    vt = qkv_t[2 * E :]
    lane = lax.broadcasted_iota(jnp.int32, (512, 256), 1)
    row = lax.broadcasted_iota(jnp.int32, (512, 256), 0)
    odd = (row // 64) % 2
    flags = jnp.where((lane == E) & (odd == 0), 1.0, jnp.where((lane == E + 1) & (odd == 1), 1.0, 0.0))
    ka = (pad_lanes(dot_nt(na, wt_ref[E : 2 * E])) + flags).astype(bf16)
    at = lax.broadcasted_iota(jnp.int32, (16, 128), 0)
    col = lax.broadcasted_iota(jnp.int32, (16, 128), 1)
    other_row = ((at == 0) & (col >= 64)) | ((at == 1) & (col < 64))
    extra = jnp.where(other_row, NEG, 0.0).astype(bf16)
    one_rows = jnp.ones((16, 128), bf16)
    if keep is not None:
        qk_ref, va_ref, p_ref = keep
        qk_ref[...] = qkv_t[: 2 * E]
        ones = jnp.where((lane == E) | (lane == E + 1), 1.0, 0.0)
        va_ref[...] = (pad_lanes(dot_nt(na, wt_ref[2 * E :])) + ones).astype(bf16)
    for p in range(4):
        cols = slice(128 * p, 128 * (p + 1))
        rhs = jnp.concatenate(
            [place(qkv_t[D * h : D * (h + 1), cols], h, extra) for h in range(H)], axis=1
        )
        scores = dot(ka[cols, : E + 16], rhs)
        top = jnp.max(scores, axis=0, keepdims=True)
        e = jnp.exp2((scores - top) * EXP2_SCALE).astype(bf16)
        for h in range(H):
            heads = slice(D * h, D * (h + 1))
            wide = slice(128 * h, 128 * (h + 1))
            out = dot(jnp.concatenate([vt[heads, cols], one_rows], axis=0), e[:, wide])
            inv = 1.0 / out[D : D + 1]
            ot_ref[heads, cols] = out[:D] * inv
            if keep is not None:
                p_ref[p, :, wide] = (e[:, wide].astype(f32) * inv).astype(bf16)


def take_rows(zhi_ref, cells_ref, cot_ref, recv_ref, x_scr):
    zhi = zhi_ref[0]
    for r in range(8):
        mine = pl.multiple_of(64 * r + 32 * zhi, 32)
        other = pl.multiple_of(64 * r + 32 * (1 - zhi), 32)
        src = pl.multiple_of(256 * zhi + 32 * r, 32)
        own = (cells_ref[pl.ds(src, 32), :].astype(f32), cot_ref[pl.ds(src, 32), :].astype(f32))
        x_scr[pl.ds(mine, 32), :] = jnp.concatenate(own, axis=1)
        x_scr[pl.ds(other, 32), :] = recv_ref[32 * r : 32 * (r + 1), :].astype(f32)


def row_forward(zhi_ref, cells_ref, cot_ref, recv_ref, wt_ref, wout_ref, mid_ref, x_scr, ot_scr):
    take_rows(zhi_ref, cells_ref, cot_ref, recv_ref, x_scr)
    x = x_scr[:, :E]
    attend(x, wt_ref, ot_scr)
    mid = x + dot(transposed(ot_scr[...]).astype(bf16), wout_ref[...])
    both = jnp.concatenate([mid, x_scr[:, E:]], axis=1).reshape(8, 64, 2 * E)
    mid_ref[...] = jnp.swapaxes(both, 0, 1).reshape(512, 2 * E).astype(bf16)


def row_again(
    zhi_ref, cells_ref, recv_ref, wt_ref, x_ref, ot_ref, qk_ref, va_ref, p_ref, x_scr, ot_scr
):
    take_rows(zhi_ref, cells_ref, cells_ref, recv_ref, x_scr)
    x = x_scr[:, :E]
    x_ref[...] = x.astype(bf16)
    attend(x, wt_ref, ot_scr, (qk_ref, va_ref, p_ref))
    ot_ref[...] = ot_scr[...].astype(bf16)


def row_backward(
    core_ref, dmid_ref, wout_ref, x_ref, ot_ref, qk_ref, va_ref, p_ref,
    both_ref, dq_ref, dk_ref, dv_ref, keep_ref, send_ref, sums_scr, dqt_scr, dk_scr, dv_scr,
):
    both = jnp.swapaxes(dmid_ref[...].astype(f32).reshape(64, 8, 2 * E), 0, 1).reshape(512, 2 * E)
    both_ref[...] = both.astype(bf16)
    dmid_low = both[:, :E].astype(bf16)
    sum_out = dot(ot_ref[...], dmid_low)
    d_att = dot_nt(wout_ref[...], dmid_low).astype(bf16)
    zero_rows = jnp.zeros((16, 128), bf16)
    for p in range(4):
        cols = slice(128 * p, 128 * (p + 1))
        blocks = []
        for h in range(H):
            heads = slice(D * h, D * (h + 1))
            d_out = d_att[heads, cols]
            delta = jnp.sum(d_out.astype(f32) * ot_ref[heads, cols].astype(f32), axis=0, keepdims=True)
            blocks.append(place(d_out, h, split_rows(delta)))
        rhs = jnp.concatenate(blocks, axis=1)
        probs = p_ref[p]
        ds = (probs.astype(f32) * dot(va_ref[cols, : E + 16], rhs)).astype(bf16)
        for h in range(H):
            heads = slice(D * h, D * (h + 1))
            dqt_scr[heads, cols] = dot(qk_ref[E + D * h : E + D * (h + 1), cols], ds[:, 128 * h : 128 * (h + 1)])
        q_rhs = jnp.concatenate(
            [place(qk_ref[D * h : D * (h + 1), cols], h, zero_rows)[:E] for h in range(H)], axis=1
        )
        dk_scr[cols, :] = dot_nt(ds, q_rhs)
        dv_scr[cols, :] = dot_nt(probs, rhs[:E])
    dq = pad_lanes((transposed(dqt_scr[...]) * SCALE).astype(bf16))
    dk = pad_lanes((dk_scr[...] * SCALE).astype(bf16))
    dv = pad_lanes(dv_scr[...].astype(bf16))
    dq_ref[...] = dq
    dk_ref[...] = dk
    dv_ref[...] = dv
    na_t = transposed(norm(x_ref[...].astype(f32))[0].astype(bf16)).astype(bf16)
    tiles = pack_tiles(dot(na_t, dq), dot(na_t, dk), dot(na_t, dv), pad_lanes(sum_out))
    for t in range(6):
        sums_scr[E * t : E * (t + 1), :] = tiles[t].astype(bf16)
    halve(core_ref, sums_scr, keep_ref, send_ref, LATE)


def cells_grad(zhi_ref, both_ref, dq_ref, dk_ref, dv_ref, x_ref, wt_ref, own_ref, other_ref, g_scr):
    zhi = zhi_ref[0]
    grad = (
        dot(dq_ref[:, :E], wt_ref[:E])
        + dot(dk_ref[:, :E], wt_ref[E : 2 * E])
        + dot(dv_ref[:, :E], wt_ref[2 * E :])
    )
    dmid = both_ref[:, :E].astype(f32)
    normed, inv_std = norm(x_ref[...].astype(f32))
    g_scr[:, :E] = dmid + norm_back(normed, inv_std, grad)
    g_scr[:, E:] = both_ref[:, E:].astype(f32)
    for r in range(8):
        mine = pl.multiple_of(64 * r + 32 * zhi, 32)
        other = pl.multiple_of(64 * r + 32 * (1 - zhi), 32)
        own_ref[32 * r : 32 * (r + 1), :] = g_scr[pl.ds(mine, 32), :].astype(bf16)
        other_ref[32 * r : 32 * (r + 1), :] = g_scr[pl.ds(other, 32), :].astype(bf16)


def column(
    core_ref, own_ref, sib_ref, bias_ref, wt_ref, wout_ref, wup_ref, wdown_ref,
    lay_ref, dmid_ref, nsib_ref, keep_ref, send_ref,
    sums_scr, ka_scr, va_scr, vt_scr, kt_scr, qt_scr, e_scr, ds_scr, qm_scr, dm_scr, ot_scr, inv_scr, dqt_scr,
):
    n = 512
    mid_own = own_ref[:, :E].astype(f32)
    normed_own, inv_own = norm(mid_own)
    normed_sib, inv_sib = norm(sib_ref[:, :E].astype(f32))
    nb_own = normed_own.astype(bf16)
    nb = jnp.concatenate([nb_own, normed_sib.astype(bf16)], axis=0)
    lane = lax.broadcasted_iota(jnp.int32, (2 * n, 256), 1)
    at = lax.broadcasted_iota(jnp.int32, (16, 256), 0)
    col = lax.broadcasted_iota(jnp.int32, (16, 256), 1)
    place_bias = jnp.where((at == 0) & (col == E), 1.0, 0.0).astype(bf16)
    bias = dot(jnp.transpose(bias_ref[...]).astype(bf16), place_bias)
    ka_scr[...] = (pad_lanes(dot_nt(nb, wt_ref[E : 2 * E])) + bias).astype(bf16)
    ones = jnp.where((lane == E) | (lane == E + 1), 1.0, 0.0)
    va_scr[...] = (pad_lanes(dot_nt(nb, wt_ref[2 * E :])) + ones).astype(bf16)
    qt_scr[...] = dot_nt(wt_ref[:E], nb_own).astype(bf16)
    kt_scr[...] = dot_nt(wt_ref[E : 2 * E], nb).astype(bf16)
    vt_scr[...] = dot_nt(wt_ref[2 * E :], nb).astype(bf16)
    one_rows = jnp.ones((16, 2 * n), bf16)
    at = lax.broadcasted_iota(jnp.int32, (16, n), 0)
    extra = jnp.where(at == 0, 1.0, 0.0).astype(bf16)
    head_lane = lax.broadcasted_iota(jnp.int32, (n, 256), 1) // D
    q_cells = pad_lanes(dot_nt(nb_own, wt_ref[:E]).astype(bf16))
    for h in range(H):
        qm_scr[n * h : n * (h + 1), :] = jnp.where(head_lane == h, q_cells, 0)

    def scores_of(h):
        return dot(ka_scr[:, : E + 16], place(qt_scr[D * h : D * (h + 1), :], h, extra))

    ahead = scores_of(0)
    for h in range(H):
        heads = slice(D * h, D * (h + 1))
        scores = ahead
        if h + 1 < H:
            ahead = scores_of(h + 1)
        top = jnp.max(scores, axis=0, keepdims=True)
        e = jnp.exp2((scores - top) * EXP2_SCALE).astype(bf16)
        e_scr[:, n * h : n * (h + 1)] = e
        out = dot(jnp.concatenate([vt_scr[heads, :], one_rows], axis=0), e)
        inv = 1.0 / out[D : D + 1]
        inv_scr[8 * h : 8 * (h + 1), :] = jnp.broadcast_to(inv, (8, n))
        ot_scr[heads, :] = out[:D] * inv
    att_t = ot_scr[...]
    mid_b = (mid_own + dot(transposed(att_t).astype(bf16), wout_ref[...])).astype(bf16).astype(f32)
    normed_c, inv_c = norm(mid_b)
    nc = normed_c.astype(bf16)
    cot = own_ref[:, E:]
    pre = dot(nc, wup_ref[...])
    square = pre * pre
    tanh = jnp.tanh(GELU_A * (pre + GELU_B * square * pre))
    half = 0.5 * (1.0 + tanh)
    hidden = (pre * half).astype(bf16)
    slope = half + 0.5 * pre * (1.0 - tanh * tanh) * (GELU_A * (1.0 + 3.0 * GELU_B * square))
    d_pre = (dot(cot, wdown_ref[...]) * slope).astype(bf16)
    lay_ref[...] = mid_b + dot_nt(hidden, wdown_ref[...])
    sum_up = dot(transposed(nc).astype(bf16), d_pre).astype(bf16)
    sum_down = dot(transposed(cot).astype(bf16), hidden).astype(bf16)
    for t in range(6):
        sums_scr[E * (6 + t) : E * (7 + t), :] = sum_up[:, 128 * t : 128 * (t + 1)]
        sums_scr[E * (12 + t) : E * (13 + t), :] = sum_down[:, 128 * t : 128 * (t + 1)]
    d_mid = cot.astype(f32) + norm_back(normed_c, inv_c, dot_nt(d_pre, wup_ref[...]))
    d_mid_low = d_mid.astype(bf16)
    sum_out = dot(att_t.astype(bf16), d_mid_low)
    d_att = dot_nt(wout_ref[...], d_mid_low).astype(bf16).astype(f32)
    d_low = []
    for h in range(H):
        heads = slice(D * h, D * (h + 1))
        d_low.append((d_att[heads] * inv_scr[8 * h : 8 * h + 1, :]).astype(bf16))
    d_cells = pad_lanes(transposed(jnp.concatenate(d_low, axis=0)).astype(bf16))
    for h in range(H):
        dm_scr[n * h : n * (h + 1), :] = jnp.where(head_lane == h, d_cells, 0)

    def dprobs_of(h):
        heads = slice(D * h, D * (h + 1))
        delta = jnp.sum(d_low[h].astype(f32) * ot_scr[heads, :], axis=0, keepdims=True)
        return dot(va_scr[:, : E + 16], place(d_low[h], h, split_rows(delta)))

    ahead = dprobs_of(0)
    for h in range(H):
        heads = slice(D * h, D * (h + 1))
        dprobs = ahead
        if h + 1 < H:
            ahead = dprobs_of(h + 1)
        ds = (e_scr[:, n * h : n * (h + 1)].astype(f32) * dprobs).astype(bf16)
        ds_scr[:, n * h : n * (h + 1)] = ds
        dqt_scr[heads, :] = dot(kt_scr[heads, :], ds)
    dq = pad_lanes((transposed(dqt_scr[...]) * SCALE).astype(bf16))
    dk = (dot(ds_scr[...], qm_scr[...]) * SCALE).astype(bf16)
    dv = dot(e_scr[...], dm_scr[...]).astype(bf16)
    nb_t = transposed(nb).astype(bf16)
    tiles = pack_tiles(dot(nb_t[:, :n], dq), dot(nb_t, dk), dot(nb_t, dv), pad_lanes(sum_out))
    for t in range(6):
        sums_scr[E * t : E * (t + 1), :] = tiles[t].astype(bf16)
    halve(core_ref, sums_scr, keep_ref, send_ref, EARLY)
    grad = dot(dk[:, :E], wt_ref[E : 2 * E]) + dot(dv[:, :E], wt_ref[2 * E :])
    grad_own = grad[:n] + dot(dq[:, :E], wt_ref[:E])
    dmid_ref[...] = d_mid_low.astype(f32) + norm_back(normed_own, inv_own, grad_own)
    nsib_ref[...] = norm_back(normed_sib, inv_sib, grad[n:]).astype(bf16)


def sum_shares(parts_ref, out_ref):
    total = jnp.sum(parts_ref[...].astype(f32), axis=0).astype(bf16)
    out_ref[...] = jnp.broadcast_to(total[None], out_ref.shape)


def join(d_own_ref, n_recv_ref, lay_ref, keep_ref, recv_ref, out_ref, early_ref):
    d_mid = d_own_ref[...] + n_recv_ref[...].astype(f32)
    out_ref[...] = jnp.concatenate([d_mid, lay_ref[...]], axis=1).astype(bf16)
    early_ref[...] = (keep_ref[...].astype(f32) + recv_ref[...].astype(f32)).astype(bf16)


def merge(early_ref, keep_ref, recv_ref, out_ref):
    out_ref[:EARLY, :] = early_ref[...]
    out_ref[EARLY : EARLY + LATE, :] = (keep_ref[...].astype(f32) + recv_ref[...].astype(f32)).astype(bf16)
    out_ref[EARLY + LATE :, :] = jnp.zeros((SHARE - EARLY - LATE, 128), bf16)


def assemble(zhi_ref, own_ref, back_ref, grad_ref, lay_ref):
    zhi = zhi_ref[0]
    for ref, at in ((own_ref, zhi), (back_ref, 1 - zhi)):
        rows = pl.ds(pl.multiple_of(256 * at, 256), 256)
        grad_ref[rows, :] = ref[:, :E]
        lay_ref[rows, :] = ref[:, E:]


def finish(core_ref, own_ref, sib_ref, qkv_f_ref, out_f_ref, qkv_s_ref, out_s_ref, up_ref, down_ref, scr):
    core = core_ref[0]
    rows = EARLY + LATE
    scr[pl.ds(pl.multiple_of(core * rows, 64), rows), :] = own_ref[:rows, :]
    scr[pl.ds(pl.multiple_of((1 - core) * rows, 64), rows), :] = sib_ref[:rows, :]
    factor = 2.0 ** -8

    def early(t):
        at = E * t if t < 9 else E * t + LATE
        return scr[at : at + E, :].astype(f32)

    def late(t):
        at = EARLY + E * t if t < 3 else 2 * EARLY + E * t
        return scr[at : at + E, :].astype(f32)

    unpack_tiles(early, qkv_s_ref, out_s_ref, factor)
    unpack_tiles(late, qkv_f_ref, out_f_ref, factor)
    for t in range(6):
        up_ref[:, 128 * t : 128 * (t + 1)] = early(6 + t) * factor
        down_ref[:, 128 * t : 128 * (t + 1)] = early(12 + t) * factor


def call(kernel, outs, scratch=(), flops=0, smem=0, name=None, mib=12, in_hbm=0, out_hbm=0, sems=0):
    vmem = pl.BlockSpec(memory_space=pltpu.VMEM)
    hbm = pl.BlockSpec(memory_space=pltpu.HBM)

    def run(*args):
        in_specs = [pl.BlockSpec(memory_space=pltpu.SMEM)] * smem + [vmem] * (len(args) - smem - in_hbm) + [hbm] * in_hbm
        moved = sum(a.size * a.dtype.itemsize for a in args) if flops else 0
        return pl.pallas_call(
            kernel,
            out_shape=[jax.ShapeDtypeStruct(s, t) for s, t in outs],
            in_specs=in_specs,
            out_specs=[vmem] * (len(outs) - out_hbm) + [hbm] * out_hbm,
            scratch_shapes=[pltpu.VMEM(s, t) for s, t in scratch] + [pltpu.SemaphoreType.DMA((sems,))] * (sems > 0),
            compiler_params=pltpu.CompilerParams(vmem_limit_bytes=mib * 1024 * 1024),
            cost_estimate=pl.CostEstimate(flops=flops, bytes_accessed=moved, transcendentals=0),
            name=name,
        )(*args)

    return run


def shards(cells, split, w_qkv_feat, w_out_feat, w_qkv_samp, w_out_samp, w_up, w_down, cotangent):
    zhi = lax.axis_index("zhi")
    core = lax.axis_index("core")
    group = ("zhi", "chip")
    swap = [(0, 1), (1, 0)]
    wf_t, ws_t = w_qkv_feat.T, w_qkv_samp.T
    zhi_arr = zhi.astype(jnp.int32).reshape(1)
    core_arr = core.astype(jnp.int32).reshape(1)

    take = lambda v: lax.dynamic_slice_in_dim(v, 8 * (1 - zhi), 8, 0).reshape(256, E)
    sent = jnp.concatenate([take(cells), take(cotangent)], axis=1)
    recv = lax.ppermute(sent, "zhi", swap)

    (mid,) = call(
        row_forward,
        [((512, 2 * E), bf16)],
        [((512, 2 * E), f32), ((E, 512), f32)],
        flops=600_000_000, smem=1, name="row_forward",
    )(zhi_arr, cells.reshape(512, E), cotangent.reshape(512, E), recv, wf_t, w_out_feat)

    train = jnp.arange(16, dtype=jnp.int32)[None, :] < split[:, None]
    bias = jnp.where(train, 0.0, NEG).astype(f32).reshape(32, 2, 2, 8).transpose(1, 2, 0, 3).reshape(2, 512)
    bias = jnp.where(core == 0, bias, bias[::-1]).reshape(1, 1024)
    bias = jnp.pad(bias, ((0, 15), (0, 0)))
    mid, bias, ws_t = lax.optimization_barrier((mid, bias, ws_t))
    own = lax.all_to_all(mid.reshape(64, 8, 2 * E), group, 0, 0, tiled=True).reshape(512, 2 * E)
    sib = lax.ppermute(own, "core", swap)

    lay, d_own, n_sib, early_keep, early_send = call(
        column,
        [((512, E), f32), ((512, E), f32), ((512, E), bf16), ((EARLY, 128), bf16), ((EARLY, 128), bf16)],
        [
            ((2 * EARLY, 128), bf16),
            ((1024, 256), bf16), ((1024, 256), bf16), ((E, 1024), bf16), ((E, 1024), bf16), ((E, 512), bf16),
            ((1024, H * 512), bf16), ((1024, H * 512), bf16), ((H * 512, 256), bf16), ((H * 512, 256), bf16),
            ((E, 512), f32), ((8 * H, 512), f32), ((E, 512), f32),
        ],
        flops=8_000_000_000, smem=1, name="column", mib=32,
    )(core_arr, own, sib, bias, ws_t, w_out_samp, w_up, w_down.T)

    n_recv = lax.ppermute(n_sib, "core", swap)
    early_recv = lax.ppermute(early_send, "core", swap)
    joined, early = call(
        join, [((512, 2 * E), bf16), ((EARLY, 128), bf16)], flops=10_000_000, name="join"
    )(d_own, n_recv, lay, early_keep, early_recv)
    joined, recv = lax.optimization_barrier((joined, recv))
    rows = lax.all_to_all(joined.reshape(64, 8, 2 * E), group, 0, 0, tiled=True).reshape(512, 2 * E)

    x, ot, qk, va, p = call(
        row_again,
        [
            ((512, E), bf16), ((E, 512), bf16), ((2 * E, 512), bf16), ((512, 256), bf16), ((4, 128, 768), bf16),
        ],
        [((512, 2 * E), f32), ((E, 512), f32)],
        smem=1, name="row_again",
    )(zhi_arr, cells.reshape(512, E), recv, wf_t)
    both, dq, dk, dv, late_keep, late_send = call(
        row_backward,
        [
            ((512, 2 * E), bf16), ((512, 256), bf16), ((512, 256), bf16), ((512, 256), bf16),
            ((LATE, 128), bf16), ((LATE, 128), bf16),
        ],
        [((2 * LATE, 128), bf16), ((E, 512), f32), ((512, E), f32), ((512, E), f32)],
        flops=1_500_000_000, smem=1, name="row_backward",
    )(core_arr, rows, w_out_feat, x, ot, qk, va, p)
    late_recv = lax.ppermute(late_send, "core", swap)
    mine, other = call(
        cells_grad, [((256, 2 * E), bf16), ((256, 2 * E), bf16)], [((512, 2 * E), f32)],
        flops=300_000_000, smem=1, name="cells_grad",
    )(zhi_arr, both, dq, dk, dv, x, wf_t)
    back = lax.ppermute(other, "zhi", swap)
    late_recv, mine = lax.optimization_barrier((late_recv, mine))
    (share,) = call(merge, [((SHARE, 128), bf16)], flops=10_000_000, name="merge")(early, late_keep, late_recv)
    parts = lax.all_to_all(share.reshape(64, CHUNK, 128), group, 0, 0, tiled=True)
    grad_cells, layer_out = call(
        assemble, [((512, E), bf16), ((512, E), bf16)], flops=100_000_000_000, smem=1, name="assemble"
    )(zhi_arr, mine, back)
    parts, grad_cells = lax.optimization_barrier((parts, grad_cells))
    (total,) = call(sum_shares, [((64, CHUNK, 128), bf16)], flops=10_000_000, name="sum_shares")(parts)
    sums = lax.all_to_all(total, group, 0, 0, tiled=True).reshape(SHARE, 128)
    sums_sib = lax.ppermute(sums, "core", swap)
    g_qkv_feat, g_out_feat, g_qkv_samp, g_out_samp, g_up, g_down_t = call(
        finish,
        [((E, 576), f32), ((E, E), f32), ((E, 576), f32), ((E, E), f32), ((E, 768), f32), ((E, 768), f32)],
        [((2 * (EARLY + LATE), 128), bf16)],
        flops=10_000_000, smem=1, name="finish",
    )(core_arr, sums, sums_sib)
    return (
        layer_out.reshape(16, 32, E), grad_cells.reshape(16, 32, E),
        g_qkv_feat, g_out_feat, g_qkv_samp, g_out_samp, g_up, g_down_t.T,
    )


def solution(mesh):
    wide = Mesh(mesh.devices.reshape(32, 2, 2), ("chip", "core", "zhi"))
    cells = P(("chip", "core"), "zhi", None)
    return jax.shard_map(
        shards,
        mesh=wide,
        in_specs=(cells, P(), P(), P(), P(), P(), P(), P(), cells),
        out_specs=(cells, cells, P(), P(), P(), P(), P(), P()),
        check_vma=False,
    )
```

```python
import jax
import jax.numpy as jnp
from jax import lax
from jax.experimental import pallas as pl
from jax.experimental.pallas import tpu as pltpu
from jax.sharding import Mesh, PartitionSpec as P

H = 6
D = 32
E = 192
EPS = 1e-05
SCALE = D ** -0.5
EXP2_SCALE = SCALE * 1.4426950408889634
NEG = -1e30
GELU_A = 0.7978845608028654
GELU_B = 0.044715
f32 = jnp.float32
bf16 = jnp.bfloat16
EARLY = 9 * E
LATE = 3 * E
CHUNK = 40
SHARE = 64 * CHUNK


def dot(a, b):
    return jnp.dot(a, b, preferred_element_type=f32)


def dot_nt(a, b):
    return lax.dot_general(a, b, (((1,), (1,)), ((), ())), preferred_element_type=f32)


def transposed(v):
    return jnp.transpose(v.astype(f32))


def lane_mean(v):
    return dot(v.astype(bf16), jnp.full((E, E), 1.0, bf16)) * (1.0 / E)


def norm(v):
    centered = v - lane_mean(v)
    inv_std = lax.rsqrt(lane_mean(centered * centered) + EPS)
    return centered * inv_std, inv_std


def norm_back(normed, inv_std, grad):
    return inv_std * (grad - lane_mean(grad) - normed * lane_mean(grad * normed))


def place(rows, head, extra=None):
    count = rows.shape[1]
    parts = []
    if head > 0:
        parts.append(jnp.zeros((D * head, count), bf16))
    parts.append(rows)
    if head < H - 1:
        parts.append(jnp.zeros((E - D * (head + 1), count), bf16))
    if extra is not None:
        parts.append(extra)
    return jnp.concatenate(parts, axis=0)


def split_rows(delta):
    high = (-delta).astype(bf16).astype(f32)
    low = -delta - high
    at = lax.broadcasted_iota(jnp.int32, (16, delta.shape[1]), 0)
    return jnp.where(at == 0, high, jnp.where(at == 1, low, 0.0)).astype(bf16)


def pack_tiles(q, k, v, out):
    lane = lax.broadcasted_iota(jnp.int32, (E, 128), 1)
    roll = lambda t: pltpu.roll(t, 64, 1)
    low = lane < 64
    return (
        q[:, :128],
        jnp.where(low, q[:, 128:], roll(k[:, :128])),
        jnp.where(low, roll(k[:, :128]), roll(k[:, 128:])),
        v[:, :128],
        out[:, :128],
        jnp.where(low, v[:, 128:], roll(out[:, 128:])),
    )


def unpack_tiles(tile, qkv_ref, out_ref, factor):
    for t in range(4):
        qkv_ref[:, 128 * t : 128 * (t + 1)] = tile(t) * factor
    last = tile(5) * factor
    qkv_ref[:, 512:576] = last[:, :64]
    out_ref[:, :128] = tile(4) * factor
    out_ref[:, 128:192] = pltpu.roll(last, 64, 1)[:, :64]


def pad_lanes(v):
    return jnp.concatenate([v, jnp.zeros((v.shape[0], 256 - E), v.dtype)], axis=1)


def halve(core_ref, sums_scr, keep_ref, send_ref, rows):
    core = core_ref[0]
    keep_ref[...] = sums_scr[pl.ds(pl.multiple_of(core * rows, 64), rows), :]
    send_ref[...] = sums_scr[pl.ds(pl.multiple_of((1 - core) * rows, 64), rows), :]


def row_masks():
    row = (lax.broadcasted_iota(jnp.int32, (D, 128 * H), 1) // 32) % 4
    return [row == i for i in range(4)]


def same_row(masks, full):
    halves = []
    for at in (0, 128):
        part = full[at + 96 : at + 128]
        for i in range(3):
            part = jnp.where(masks[i], full[at + 32 * i : at + 32 * (i + 1)], part)
        halves.append(part)
    return jnp.concatenate(halves, axis=0)


def spread(masks, part):
    parts = [jnp.where(mask, part[at : at + D], 0.0) for at in (0, D) for mask in masks]
    return jnp.concatenate(parts, axis=0).astype(bf16)


def grouped(cells_ref, recv_ref):
    parts = [ref[128 * p : 128 * (p + 1), :] for p in range(4) for ref in (cells_ref, recv_ref)]
    return jnp.concatenate(parts, axis=0).astype(f32)


def own_lanes(v):
    return jnp.concatenate([v[:, 256 * p : 256 * p + 128] for p in range(4)], axis=1)


def attend(cells_ref, recv_ref, wt_ref, ot_ref, keep=None):
    masks = row_masks()
    one_rows = jnp.ones((16, 256), bf16)
    na = norm(grouped(cells_ref, recv_ref))[0].astype(bf16)
    qt = own_lanes(dot_nt(wt_ref[:E], na).astype(bf16))
    keys = dot_nt(na, wt_ref[E : 2 * E]).astype(bf16)
    vt = dot_nt(wt_ref[2 * E : 3 * E], na).astype(bf16)
    if keep is not None:
        na_ref, qt_ref, kt_ref, p_ref = keep
        na_ref[...] = na
        qt_ref[...] = qt
        kt_ref[...] = dot_nt(wt_ref[E : 2 * E], na).astype(bf16)
    for p in range(4):
        cols = slice(128 * p, 128 * (p + 1))
        both = slice(256 * p, 256 * (p + 1))
        rhs = jnp.concatenate([place(qt[D * h : D * (h + 1), cols], h) for h in range(H)], axis=1)
        scores = same_row(masks, dot(keys[both], rhs))
        e = jnp.exp2((scores - jnp.max(scores, axis=0, keepdims=True)) * EXP2_SCALE)
        wide_e = spread(masks, e)
        invs = []
        for h in range(H):
            heads = slice(D * h, D * (h + 1))
            wide = slice(128 * h, 128 * (h + 1))
            out = dot(jnp.concatenate([vt[heads, both], one_rows], axis=0), wide_e[:, wide])
            inv = 1.0 / out[D : D + 1]
            invs.append(inv)
            ot_ref[heads, cols] = out[:D] * inv
        if keep is not None:
            p_ref[p] = (e * jnp.concatenate(invs, axis=1)).astype(bf16)


def row_forward(cells_ref, cot_ref, recv_ref, wt_ref, mid_ref, ot_scr):
    attend(cells_ref, recv_ref, wt_ref, ot_scr)
    mid = cells_ref[...].astype(f32) + dot(transposed(ot_scr[...]).astype(bf16), wt_ref[3 * E :])
    both = jnp.concatenate([mid, cot_ref[...].astype(f32)], axis=1).reshape(16, 32, 2 * E)
    mid_ref[...] = jnp.swapaxes(both, 0, 1).reshape(512, 2 * E).astype(bf16)


def row_again(cells_ref, recv_ref, wt_ref, ot_ref, *rest):
    keep, ot_scr = rest[:-1], rest[-1]
    attend(cells_ref, recv_ref, wt_ref, ot_scr, keep)
    ot_ref[...] = ot_scr[...].astype(bf16)


def row_backward(
    core_ref, rows_ref, wt_ref, ot_ref, na_ref, qt_ref, kt_ref, p_ref,
    lay_ref, dmid_ref, dq_ref, dk_ref, dv_ref, keep_ref, send_ref, sums_scr, dqt_scr, dk_scr, dv_scr,
):
    both = jnp.swapaxes(rows_ref[...].astype(f32).reshape(32, 16, 2 * E), 0, 1).reshape(512, 2 * E)
    lay_ref[...] = both[:, E:].astype(bf16)
    dmid_ref[...] = both[:, :E]
    dmid_low = both[:, :E].astype(bf16)
    sum_out = dot(ot_ref[...], dmid_low)
    d_att = dot_nt(wt_ref[3 * E :], dmid_low).astype(bf16)
    na = na_ref[...]
    lane = lax.broadcasted_iota(jnp.int32, (1024, 256), 1)
    ones = jnp.where((lane == E) | (lane == E + 1), 1.0, 0.0)
    va = (pad_lanes(dot_nt(na, wt_ref[2 * E : 3 * E])) + ones).astype(bf16)
    masks = row_masks()
    for p in range(4):
        cols = slice(128 * p, 128 * (p + 1))
        both = slice(256 * p, 256 * (p + 1))
        blocks = []
        for h in range(H):
            heads = slice(D * h, D * (h + 1))
            d_out = d_att[heads, cols]
            delta = jnp.sum(d_out.astype(f32) * ot_ref[heads, cols].astype(f32), axis=0, keepdims=True)
            blocks.append(place(d_out, h, split_rows(delta)))
        rhs = jnp.concatenate(blocks, axis=1)
        q_rhs = jnp.concatenate([place(qt_ref[D * h : D * (h + 1), cols], h) for h in range(H)], axis=1)
        part = p_ref[p].astype(f32)
        ds = spread(masks, part * same_row(masks, dot(va[both, : E + 16], rhs)))
        dk_scr[both, :] = dot_nt(ds, q_rhs)
        dv_scr[both, :] = dot_nt(spread(masks, part), rhs[:E])
        for h in range(H):
            heads = slice(D * h, D * (h + 1))
            dqt_scr[heads, cols] = dot(kt_ref[heads, both], ds[:, 128 * h : 128 * (h + 1)])
    dq = pad_lanes((transposed(dqt_scr[...]) * SCALE).astype(bf16))
    dk = pad_lanes((dk_scr[...] * SCALE).astype(bf16))
    dv = pad_lanes(dv_scr[...].astype(bf16))
    dq_ref[...] = dq
    dk_ref[...] = dk
    dv_ref[...] = dv
    na_t = transposed(na).astype(bf16)
    tiles = pack_tiles(dot(own_lanes(na_t), dq), dot(na_t, dk), dot(na_t, dv), pad_lanes(sum_out))
    for t in range(6):
        sums_scr[E * t : E * (t + 1), :] = tiles[t].astype(bf16)
    halve(core_ref, sums_scr, keep_ref, send_ref, LATE)


def cells_grad(dmid_ref, dq_ref, dk_ref, dv_ref, cells_ref, recv_ref, wt_ref, own_ref, other_ref):
    grad = dot(dk_ref[:, :E], wt_ref[E : 2 * E]) + dot(dv_ref[:, :E], wt_ref[2 * E : 3 * E])
    split = [jnp.concatenate([grad[256 * p + at : 256 * p + at + 128] for p in range(4)], axis=0) for at in (0, 128)]
    normed, inv_std = norm(recv_ref[...].astype(f32))
    other_ref[...] = norm_back(normed, inv_std, split[1]).astype(bf16)
    normed, inv_std = norm(cells_ref[...].astype(f32))
    own_ref[...] = dmid_ref[...] + norm_back(normed, inv_std, split[0] + dot(dq_ref[:, :E], wt_ref[:E]))


def column(
    core_ref, own_ref, sib_ref, bias_ref, wt_ref, wup_ref, wdown_ref,
    lay_ref, dmid_ref, nsib_ref, keep_ref, send_ref,
    sums_scr, ka_scr, va_scr, vt_scr, kt_scr, qt_scr, e_scr, ds_scr, qm_scr, dm_scr, ot_scr, inv_scr, dqt_scr,
):
    n = 512
    mid_own = own_ref[:, :E].astype(f32)
    normed_own, inv_own = norm(mid_own)
    normed_sib, inv_sib = norm(sib_ref[:, :E].astype(f32))
    nb_own = normed_own.astype(bf16)
    nb = jnp.concatenate([nb_own, normed_sib.astype(bf16)], axis=0)
    lane = lax.broadcasted_iota(jnp.int32, (2 * n, 256), 1)
    at = lax.broadcasted_iota(jnp.int32, (16, 256), 0)
    col = lax.broadcasted_iota(jnp.int32, (16, 256), 1)
    place_bias = jnp.where((at == 0) & (col == E), 1.0, 0.0).astype(bf16)
    bias = dot(jnp.transpose(bias_ref[...]).astype(bf16), place_bias)
    ka_scr[...] = (pad_lanes(dot_nt(nb, wt_ref[E : 2 * E])) + bias).astype(bf16)
    ones = jnp.where((lane == E) | (lane == E + 1), 1.0, 0.0)
    va_scr[...] = (pad_lanes(dot_nt(nb, wt_ref[2 * E : 3 * E])) + ones).astype(bf16)
    qt_scr[...] = dot_nt(wt_ref[:E], nb_own).astype(bf16)
    kt_scr[...] = dot_nt(wt_ref[E : 2 * E], nb).astype(bf16)
    vt_scr[...] = dot_nt(wt_ref[2 * E : 3 * E], nb).astype(bf16)
    one_rows = jnp.ones((16, 2 * n), bf16)
    at = lax.broadcasted_iota(jnp.int32, (16, n), 0)
    extra = jnp.where(at == 0, 1.0, 0.0).astype(bf16)
    head_lane = lax.broadcasted_iota(jnp.int32, (n, 256), 1) // D
    q_cells = pad_lanes(dot_nt(nb_own, wt_ref[:E]).astype(bf16))
    for h in range(H):
        qm_scr[n * h : n * (h + 1), :] = jnp.where(head_lane == h, q_cells, 0)

    def scores_of(h):
        return dot(ka_scr[:, : E + 16], place(qt_scr[D * h : D * (h + 1), :], h, extra))

    ahead = scores_of(0)
    for h in range(H):
        heads = slice(D * h, D * (h + 1))
        scores = ahead
        if h + 1 < H:
            ahead = scores_of(h + 1)
        top = jnp.max(scores, axis=0, keepdims=True)
        e = jnp.exp2((scores - top) * EXP2_SCALE).astype(bf16)
        e_scr[:, n * h : n * (h + 1)] = e
        out = dot(jnp.concatenate([vt_scr[heads, :], one_rows], axis=0), e)
        inv = 1.0 / out[D : D + 1]
        inv_scr[8 * h : 8 * (h + 1), :] = jnp.broadcast_to(inv, (8, n))
        ot_scr[heads, :] = out[:D] * inv
    att_t = ot_scr[...]
    mid_b = (mid_own + dot(transposed(att_t).astype(bf16), wt_ref[3 * E :])).astype(bf16).astype(f32)
    normed_c, inv_c = norm(mid_b)
    nc = normed_c.astype(bf16)
    cot = own_ref[:, E:]
    pre = dot(nc, wup_ref[...])
    square = pre * pre
    tanh = jnp.tanh(GELU_A * (pre + GELU_B * square * pre))
    half = 0.5 * (1.0 + tanh)
    hidden = (pre * half).astype(bf16)
    slope = half + 0.5 * pre * (1.0 - tanh * tanh) * (GELU_A * (1.0 + 3.0 * GELU_B * square))
    d_pre = (dot(cot, wdown_ref[...]) * slope).astype(bf16)
    lay_ref[...] = mid_b + dot_nt(hidden, wdown_ref[...])
    sum_up = dot(transposed(nc).astype(bf16), d_pre).astype(bf16)
    sum_down = dot(transposed(cot).astype(bf16), hidden).astype(bf16)
    for t in range(6):
        sums_scr[E * (6 + t) : E * (7 + t), :] = sum_up[:, 128 * t : 128 * (t + 1)]
        sums_scr[E * (12 + t) : E * (13 + t), :] = sum_down[:, 128 * t : 128 * (t + 1)]
    d_mid = cot.astype(f32) + norm_back(normed_c, inv_c, dot_nt(d_pre, wup_ref[...]))
    d_mid_low = d_mid.astype(bf16)
    sum_out = dot(att_t.astype(bf16), d_mid_low)
    d_att = dot_nt(wt_ref[3 * E :], d_mid_low).astype(bf16).astype(f32)
    d_low = []
    for h in range(H):
        heads = slice(D * h, D * (h + 1))
        d_low.append((d_att[heads] * inv_scr[8 * h : 8 * h + 1, :]).astype(bf16))
    d_cells = pad_lanes(transposed(jnp.concatenate(d_low, axis=0)).astype(bf16))
    for h in range(H):
        dm_scr[n * h : n * (h + 1), :] = jnp.where(head_lane == h, d_cells, 0)

    def dprobs_of(h):
        heads = slice(D * h, D * (h + 1))
        delta = jnp.sum(d_low[h].astype(f32) * ot_scr[heads, :], axis=0, keepdims=True)
        return dot(va_scr[:, : E + 16], place(d_low[h], h, split_rows(delta)))

    ahead = dprobs_of(0)
    for h in range(H):
        heads = slice(D * h, D * (h + 1))
        dprobs = ahead
        if h + 1 < H:
            ahead = dprobs_of(h + 1)
        ds = (e_scr[:, n * h : n * (h + 1)].astype(f32) * dprobs).astype(bf16)
        ds_scr[:, n * h : n * (h + 1)] = ds
        dqt_scr[heads, :] = dot(kt_scr[heads, :], ds)
    dq = pad_lanes((transposed(dqt_scr[...]) * SCALE).astype(bf16))
    dk = (dot(ds_scr[...], qm_scr[...]) * SCALE).astype(bf16)
    dv = dot(e_scr[...], dm_scr[...]).astype(bf16)
    nb_t = transposed(nb).astype(bf16)
    tiles = pack_tiles(dot(nb_t[:, :n], dq), dot(nb_t, dk), dot(nb_t, dv), pad_lanes(sum_out))
    for t in range(6):
        sums_scr[E * t : E * (t + 1), :] = tiles[t].astype(bf16)
    halve(core_ref, sums_scr, keep_ref, send_ref, EARLY)
    grad = dot(dk[:, :E], wt_ref[E : 2 * E]) + dot(dv[:, :E], wt_ref[2 * E : 3 * E])
    grad_own = grad[:n] + dot(dq[:, :E], wt_ref[:E])
    dmid_ref[...] = d_mid_low.astype(f32) + norm_back(normed_own, inv_own, grad_own)
    nsib_ref[...] = norm_back(normed_sib, inv_sib, grad[n:]).astype(bf16)


def sum_shares(parts_ref, out_ref):
    total = jnp.sum(parts_ref[...].astype(f32), axis=0).astype(bf16)
    out_ref[...] = jnp.broadcast_to(total[None], out_ref.shape)


def join(d_own_ref, n_recv_ref, lay_ref, keep_ref, recv_ref, out_ref, early_ref):
    d_mid = d_own_ref[...] + n_recv_ref[...].astype(f32)
    out_ref[...] = jnp.concatenate([d_mid, lay_ref[...]], axis=1).astype(bf16)
    early_ref[...] = (keep_ref[...].astype(f32) + recv_ref[...].astype(f32)).astype(bf16)


def merge(early_ref, keep_ref, recv_ref, out_ref):
    out_ref[:EARLY, :] = early_ref[...]
    out_ref[EARLY : EARLY + LATE, :] = (keep_ref[...].astype(f32) + recv_ref[...].astype(f32)).astype(bf16)
    out_ref[EARLY + LATE :, :] = jnp.zeros((SHARE - EARLY - LATE, 128), bf16)


def assemble(own_ref, back_ref, grad_ref):
    grad_ref[...] = (own_ref[...] + back_ref[...].astype(f32)).astype(bf16)


def finish(core_ref, own_ref, sib_ref, qkv_f_ref, out_f_ref, qkv_s_ref, out_s_ref, up_ref, down_ref, scr):
    core = core_ref[0]
    rows = EARLY + LATE
    scr[pl.ds(pl.multiple_of(core * rows, 64), rows), :] = own_ref[:rows, :]
    scr[pl.ds(pl.multiple_of((1 - core) * rows, 64), rows), :] = sib_ref[:rows, :]
    factor = 2.0 ** -8

    def early(t):
        at = E * t if t < 9 else E * t + LATE
        return scr[at : at + E, :].astype(f32)

    def late(t):
        at = EARLY + E * t if t < 3 else 2 * EARLY + E * t
        return scr[at : at + E, :].astype(f32)

    unpack_tiles(early, qkv_s_ref, out_s_ref, factor)
    unpack_tiles(late, qkv_f_ref, out_f_ref, factor)
    for t in range(6):
        up_ref[:, 128 * t : 128 * (t + 1)] = early(6 + t) * factor
        down_ref[:, 128 * t : 128 * (t + 1)] = early(12 + t) * factor


def call(kernel, outs, scratch=(), flops=0, smem=0, name=None, mib=12, in_hbm=0, out_hbm=0, sems=0):
    vmem = pl.BlockSpec(memory_space=pltpu.VMEM)
    hbm = pl.BlockSpec(memory_space=pltpu.HBM)

    def run(*args):
        in_specs = [pl.BlockSpec(memory_space=pltpu.SMEM)] * smem + [vmem] * (len(args) - smem - in_hbm) + [hbm] * in_hbm
        moved = sum(a.size * a.dtype.itemsize for a in args) if flops else 0
        return pl.pallas_call(
            kernel,
            out_shape=[jax.ShapeDtypeStruct(s, t) for s, t in outs],
            in_specs=in_specs,
            out_specs=[vmem] * (len(outs) - out_hbm) + [hbm] * out_hbm,
            scratch_shapes=[pltpu.VMEM(s, t) for s, t in scratch] + [pltpu.SemaphoreType.DMA((sems,))] * (sems > 0),
            compiler_params=pltpu.CompilerParams(vmem_limit_bytes=mib * 1024 * 1024),
            cost_estimate=pl.CostEstimate(flops=flops, bytes_accessed=moved, transcendentals=0),
            name=name,
        )(*args)

    return run


def shards(cells, split, w_qkv_feat, w_out_feat, w_qkv_samp, w_out_samp, w_up, w_down, cotangent):
    core = lax.axis_index("core")
    group = ("zhi", "chip")
    swap = [(0, 1), (1, 0)]
    wf_t = jnp.concatenate([w_qkv_feat.T, w_out_feat], axis=0)
    ws_t = jnp.concatenate([w_qkv_samp.T, w_out_samp], axis=0)
    core_arr = core.astype(jnp.int32).reshape(1)
    cells = cells.reshape(512, E)

    recv = lax.ppermute(cells, "zhi", swap)
    (mid,) = call(
        row_forward, [((512, 2 * E), bf16)], [((E, 512), f32)], flops=900_000_000, name="row_forward"
    )(cells, cotangent.reshape(512, E), recv, wf_t)

    train = jnp.arange(16, dtype=jnp.int32)[None, :] < split[:, None]
    bias = jnp.where(train, 0.0, NEG).astype(f32).reshape(32, 2, 16).transpose(1, 0, 2).reshape(2, 512)
    bias = jnp.where(core == 0, bias, bias[::-1]).reshape(1, 1024)
    bias = jnp.pad(bias, ((0, 15), (0, 0)))
    mid, bias, ws_t = lax.optimization_barrier((mid, bias, ws_t))
    own = lax.all_to_all(mid.reshape(32, 16, 2 * E), "chip", 0, 0, tiled=True).reshape(512, 2 * E)
    sib = lax.ppermute(own, "core", swap)

    lay, d_own, n_sib, early_keep, early_send = call(
        column,
        [((512, E), f32), ((512, E), f32), ((512, E), bf16), ((EARLY, 128), bf16), ((EARLY, 128), bf16)],
        [
            ((2 * EARLY, 128), bf16),
            ((1024, 256), bf16), ((1024, 256), bf16), ((E, 1024), bf16), ((E, 1024), bf16), ((E, 512), bf16),
            ((1024, H * 512), bf16), ((1024, H * 512), bf16), ((H * 512, 256), bf16), ((H * 512, 256), bf16),
            ((E, 512), f32), ((8 * H, 512), f32), ((E, 512), f32),
        ],
        flops=8_000_000_000, smem=1, name="column", mib=32,
    )(core_arr, own, sib, bias, ws_t, w_up, w_down.T)

    n_recv = lax.ppermute(n_sib, "core", swap)
    early_recv = lax.ppermute(early_send, "core", swap)
    joined, early = call(
        join, [((512, 2 * E), bf16), ((EARLY, 128), bf16)], flops=10_000_000, name="join"
    )(d_own, n_recv, lay, early_keep, early_recv)
    joined, recv = lax.optimization_barrier((joined, recv))
    rows = lax.all_to_all(joined.reshape(32, 16, 2 * E), "chip", 0, 0, tiled=True).reshape(512, 2 * E)

    saved = call(
        row_again,
        [
            ((E, 512), bf16), ((1024, E), bf16), ((E, 512), bf16), ((E, 1024), bf16), ((4, 2 * D, 768), bf16),
        ],
        [((E, 512), f32)],
        name="row_again",
    )(cells, recv, wf_t)

    layer_out, dmid, dq, dk, dv, late_keep, late_send = call(
        row_backward,
        [
            ((512, E), bf16), ((512, E), f32), ((512, 256), bf16), ((1024, 256), bf16), ((1024, 256), bf16),
            ((LATE, 128), bf16), ((LATE, 128), bf16),
        ],
        [((2 * LATE, 128), bf16), ((E, 512), f32), ((1024, E), f32), ((1024, E), f32)],
        flops=1_500_000_000, smem=1, name="row_backward",
    )(core_arr, rows, wf_t, *saved)
    late_recv = lax.ppermute(late_send, "core", swap)
    mine, other = call(
        cells_grad, [((512, E), f32), ((512, E), bf16)], flops=20_000_000_000, name="cells_grad"
    )(dmid, dq, dk, dv, cells, recv, wf_t)
    back = lax.ppermute(other, "zhi", swap)
    late_recv, mine = lax.optimization_barrier((late_recv, mine))
    (share,) = call(merge, [((SHARE, 128), bf16)], flops=100_000_000_000, name="merge")(early, late_keep, late_recv)
    parts = lax.all_to_all(share.reshape(64, CHUNK, 128), group, 0, 0, tiled=True)
    (grad_cells,) = call(assemble, [((512, E), bf16)], flops=100_000_000_000, name="assemble")(mine, back)
    parts, grad_cells = lax.optimization_barrier((parts, grad_cells))
    (total,) = call(sum_shares, [((64, CHUNK, 128), bf16)], flops=10_000_000, name="sum_shares")(parts)
    sums = lax.all_to_all(total, group, 0, 0, tiled=True).reshape(SHARE, 128)
    sums_sib = lax.ppermute(sums, "core", swap)
    g_qkv_feat, g_out_feat, g_qkv_samp, g_out_samp, g_up, g_down_t = call(
        finish,
        [((E, 576), f32), ((E, E), f32), ((E, 576), f32), ((E, E), f32), ((E, 768), f32), ((E, 768), f32)],
        [((2 * (EARLY + LATE), 128), bf16)],
        flops=10_000_000, smem=1, name="finish",
    )(core_arr, sums, sums_sib)
    return (
        layer_out.reshape(16, 32, E), grad_cells.reshape(16, 32, E),
        g_qkv_feat, g_out_feat, g_qkv_samp, g_out_samp, g_up, g_down_t.T,
    )


def solution(mesh):
    wide = Mesh(mesh.devices.reshape(32, 2, 2), ("chip", "core", "zhi"))
    cells = P(("chip", "core"), "zhi", None)
    return jax.shard_map(
        shards,
        mesh=wide,
        in_specs=(cells, P(), P(), P(), P(), P(), P(), P(), cells),
        out_specs=(cells, cells, P(), P(), P(), P(), P(), P()),
        check_vma=False,
    )
```

```python
import jax
import jax.numpy as jnp
from jax import lax
from jax.experimental import pallas as pl
from jax.experimental.pallas import tpu as pltpu
from jax.sharding import Mesh, PartitionSpec as P

H = 6
D = 32
E = 192
EPS = 1e-05
SCALE = D ** -0.5
EXP2_SCALE = SCALE * 1.4426950408889634
NEG = -1e30
GELU_A = 0.7978845608028654
GELU_B = 0.044715
f32 = jnp.float32
bf16 = jnp.bfloat16
EARLY = 9 * E
LATE = 3 * E
CHUNK = 40
SHARE = 64 * CHUNK


def dot(a, b):
    return jnp.dot(a, b, preferred_element_type=f32)


def dot_nt(a, b):
    return lax.dot_general(a, b, (((1,), (1,)), ((), ())), preferred_element_type=f32)


def transposed(v):
    return jnp.transpose(v)


def lane_mean(v):
    return dot(v.astype(bf16), jnp.full((E, E), 1.0, bf16)) * (1.0 / E)


def norm(v):
    centered = v - lane_mean(v)
    inv_std = lax.rsqrt(lane_mean(centered * centered) + EPS)
    return centered * inv_std, inv_std


def norm_back(normed, inv_std, grad):
    return inv_std * (grad - lane_mean(grad) - normed * lane_mean(grad * normed))


def place(rows, head, extra=None):
    count = rows.shape[1]
    parts = []
    if head > 0:
        parts.append(jnp.zeros((D * head, count), bf16))
    parts.append(rows)
    if head < H - 1:
        parts.append(jnp.zeros((E - D * (head + 1), count), bf16))
    if extra is not None:
        parts.append(extra)
    return jnp.concatenate(parts, axis=0)


def split_rows(delta):
    high = (-delta).astype(bf16).astype(f32)
    low = -delta - high
    at = lax.broadcasted_iota(jnp.int32, (16, delta.shape[1]), 0)
    return jnp.where(at == 0, high, jnp.where(at == 1, low, 0.0)).astype(bf16)


def pack_tiles(q, k, v, out):
    lane = lax.broadcasted_iota(jnp.int32, (E, 128), 1)
    roll = lambda t: pltpu.roll(t, 64, 1)
    low = lane < 64
    return (
        q[:, :128],
        jnp.where(low, q[:, 128:], roll(k[:, :128])),
        jnp.where(low, roll(k[:, :128]), roll(k[:, 128:])),
        v[:, :128],
        out[:, :128],
        jnp.where(low, v[:, 128:], roll(out[:, 128:])),
    )


def unpack_tiles(tile, qkv_ref, out_ref, factor):
    for t in range(4):
        qkv_ref[:, 128 * t : 128 * (t + 1)] = tile(t) * factor
    last = tile(5) * factor
    qkv_ref[:, 512:576] = last[:, :64]
    out_ref[:, :128] = tile(4) * factor
    out_ref[:, 128:192] = pltpu.roll(last, 64, 1)[:, :64]


def pad_lanes(v):
    return jnp.concatenate([v, jnp.zeros((v.shape[0], 256 - E), v.dtype)], axis=1)


def halve(core_ref, sums_scr, keep_ref, send_ref, rows):
    core = core_ref[0]
    keep_ref[...] = sums_scr[pl.ds(pl.multiple_of(core * rows, 64), rows), :]
    send_ref[...] = sums_scr[pl.ds(pl.multiple_of((1 - core) * rows, 64), rows), :]


def row_masks():
    row = (lax.broadcasted_iota(jnp.int32, (D, 128 * H), 1) // 32) % 4
    return [row == i for i in range(4)]


def same_row(masks, full):
    halves = []
    for at in (0, 128):
        part = full[at + 96 : at + 128]
        for i in range(3):
            part = jnp.where(masks[i], full[at + 32 * i : at + 32 * (i + 1)], part)
        halves.append(part)
    return jnp.concatenate(halves, axis=0)


def spread(masks, part):
    parts = [jnp.where(mask, part[at : at + D], 0.0) for at in (0, D) for mask in masks]
    return jnp.concatenate(parts, axis=0).astype(bf16)


def grouped(cells_ref, recv_ref):
    parts = [ref[128 * p : 128 * (p + 1), :] for p in range(4) for ref in (cells_ref, recv_ref)]
    return jnp.concatenate(parts, axis=0).astype(f32)


def own_lanes(v):
    return jnp.concatenate([v[:, 256 * p : 256 * p + 128] for p in range(4)], axis=1)


def attend(cells_ref, recv_ref, wt_ref, ot_ref, keep=None):
    masks = row_masks()
    one_rows = jnp.ones((16, 256), bf16)
    na = norm(grouped(cells_ref, recv_ref))[0].astype(bf16)
    qt = own_lanes(dot_nt(wt_ref[:E], na).astype(bf16))
    keys = dot_nt(na, wt_ref[E : 2 * E]).astype(bf16)
    vt = dot_nt(wt_ref[2 * E : 3 * E], na).astype(bf16)
    if keep is not None:
        na_ref, qt_ref, kt_ref, p_ref = keep
        na_ref[...] = na
        qt_ref[...] = qt
        kt_ref[...] = dot_nt(wt_ref[E : 2 * E], na).astype(bf16)
    for p in range(4):
        cols = slice(128 * p, 128 * (p + 1))
        both = slice(256 * p, 256 * (p + 1))
        rhs = jnp.concatenate([place(qt[D * h : D * (h + 1), cols], h) for h in range(H)], axis=1)
        scores = same_row(masks, dot(keys[both], rhs))
        e = jnp.exp2((scores - jnp.max(scores, axis=0, keepdims=True)) * EXP2_SCALE)
        wide_e = spread(masks, e)
        invs = []
        for h in range(H):
            heads = slice(D * h, D * (h + 1))
            wide = slice(128 * h, 128 * (h + 1))
            out = dot(jnp.concatenate([vt[heads, both], one_rows], axis=0), wide_e[:, wide])
            inv = 1.0 / out[D : D + 1]
            invs.append(inv)
            ot_ref[heads, cols] = out[:D] * inv
        if keep is not None:
            p_ref[p] = (e * jnp.concatenate(invs, axis=1)).astype(bf16)


def row_forward(cells_ref, cot_ref, recv_ref, wt_ref, mid_ref, ot_scr):
    attend(cells_ref, recv_ref, wt_ref, ot_scr)
    mid = cells_ref[...].astype(f32) + dot(transposed(ot_scr[...]).astype(bf16), wt_ref[3 * E :])
    both = jnp.concatenate([mid, cot_ref[...].astype(f32)], axis=1).reshape(16, 32, 2 * E)
    mid_ref[...] = jnp.swapaxes(both, 0, 1).reshape(512, 2 * E).astype(bf16)


def row_again(cells_ref, recv_ref, wt_ref, ot_ref, *rest):
    keep, ot_scr = rest[:-1], rest[-1]
    attend(cells_ref, recv_ref, wt_ref, ot_scr, keep)
    ot_ref[...] = ot_scr[...].astype(bf16)


def row_backward(
    core_ref, rows_ref, wt_ref, ot_ref, na_ref, qt_ref, kt_ref, p_ref,
    lay_ref, dmid_ref, dq_ref, dk_ref, dv_ref, keep_ref, send_ref, sums_scr, dqt_scr, dk_scr, dv_scr,
):
    both = jnp.swapaxes(rows_ref[...].astype(f32).reshape(32, 16, 2 * E), 0, 1).reshape(512, 2 * E)
    lay_ref[...] = both[:, E:].astype(bf16)
    dmid_ref[...] = both[:, :E]
    dmid_low = both[:, :E].astype(bf16)
    d_att = dot_nt(wt_ref[3 * E :], dmid_low).astype(bf16)
    na = na_ref[...]
    lane = lax.broadcasted_iota(jnp.int32, (1024, 256), 1)
    ones = jnp.where((lane == E) | (lane == E + 1), 1.0, 0.0)
    va = (pad_lanes(dot_nt(na, wt_ref[2 * E : 3 * E])) + ones).astype(bf16)
    masks = row_masks()
    for p in range(4):
        cols = slice(128 * p, 128 * (p + 1))
        both = slice(256 * p, 256 * (p + 1))
        blocks = []
        for h in range(H):
            heads = slice(D * h, D * (h + 1))
            d_out = d_att[heads, cols]
            delta = jnp.sum(d_out.astype(f32) * ot_ref[heads, cols].astype(f32), axis=0, keepdims=True)
            blocks.append(place(d_out, h, split_rows(delta)))
        rhs = jnp.concatenate(blocks, axis=1)
        q_rhs = jnp.concatenate([place(qt_ref[D * h : D * (h + 1), cols], h) for h in range(H)], axis=1)
        if p == 0:
            na_t = transposed(na).astype(bf16)
        if p == 2:
            sum_out = dot(ot_ref[...], dmid_low)
        part = p_ref[p].astype(f32)
        ds = spread(masks, part * same_row(masks, dot(va[both, : E + 16], rhs)))
        dk_scr[both, :] = dot_nt(ds, q_rhs)
        dv_scr[both, :] = dot_nt(spread(masks, part), rhs[:E])
        for h in range(H):
            heads = slice(D * h, D * (h + 1))
            dqt_scr[heads, cols] = dot(kt_ref[heads, both], ds[:, 128 * h : 128 * (h + 1)])
    dq = pad_lanes((transposed(dqt_scr[...]) * SCALE).astype(bf16))
    dk = pad_lanes((dk_scr[...] * SCALE).astype(bf16))
    dv = pad_lanes(dv_scr[...].astype(bf16))
    dq_ref[...] = dq
    dk_ref[...] = dk
    dv_ref[...] = dv
    tiles = pack_tiles(dot(own_lanes(na_t), dq), dot(na_t, dk), dot(na_t, dv), pad_lanes(sum_out))
    for t in range(6):
        sums_scr[E * t : E * (t + 1), :] = tiles[t].astype(bf16)
    halve(core_ref, sums_scr, keep_ref, send_ref, LATE)


def cells_grad(dmid_ref, dq_ref, dk_ref, dv_ref, cells_ref, recv_ref, wt_ref, own_ref, other_ref):
    grad = dot(dk_ref[:, :E], wt_ref[E : 2 * E]) + dot(dv_ref[:, :E], wt_ref[2 * E : 3 * E])
    split = [jnp.concatenate([grad[256 * p + at : 256 * p + at + 128] for p in range(4)], axis=0) for at in (0, 128)]
    normed, inv_std = norm(recv_ref[...].astype(f32))
    other_ref[...] = norm_back(normed, inv_std, split[1]).astype(bf16)
    normed, inv_std = norm(cells_ref[...].astype(f32))
    own_ref[...] = dmid_ref[...] + norm_back(normed, inv_std, split[0] + dot(dq_ref[:, :E], wt_ref[:E]))


def column(
    core_ref, own_ref, sib_ref, bias_ref, wt_ref, wup_ref, wdown_ref,
    lay_ref, dmid_ref, nsib_ref, keep_ref, send_ref,
    sums_scr, ka_scr, va_scr, vt_scr, kt_scr, qt_scr, e_scr, ds_scr, qm_scr, dm_scr, ot_scr, inv_scr, dqt_scr,
):
    n = 512
    mid_own = own_ref[:, :E].astype(f32)
    normed_own, inv_own = norm(mid_own)
    normed_sib, inv_sib = norm(sib_ref[:, :E].astype(f32))
    nb_own = normed_own.astype(bf16)
    nb = jnp.concatenate([nb_own, normed_sib.astype(bf16)], axis=0)
    lane = lax.broadcasted_iota(jnp.int32, (2 * n, 256), 1)
    at = lax.broadcasted_iota(jnp.int32, (16, 256), 0)
    col = lax.broadcasted_iota(jnp.int32, (16, 256), 1)
    place_bias = jnp.where((at == 0) & (col == E), 1.0, 0.0).astype(bf16)
    bias = dot(jnp.transpose(bias_ref[...]).astype(bf16), place_bias)
    ka_scr[...] = (pad_lanes(dot_nt(nb, wt_ref[E : 2 * E])) + bias).astype(bf16)
    qt_scr[...] = dot_nt(wt_ref[:E], nb_own).astype(bf16)
    vt_scr[...] = dot_nt(wt_ref[2 * E : 3 * E], nb).astype(bf16)
    one_rows = jnp.ones((16, 2 * n), bf16)
    at = lax.broadcasted_iota(jnp.int32, (16, n), 0)
    extra = jnp.where(at == 0, 1.0, 0.0).astype(bf16)
    head_lane = lax.broadcasted_iota(jnp.int32, (n, 256), 1) // D

    def scores_of(h):
        return dot(ka_scr[:, : E + 16], place(qt_scr[D * h : D * (h + 1), :], h, extra))

    ahead = scores_of(0)
    for h in range(H):
        heads = slice(D * h, D * (h + 1))
        scores = ahead
        if h + 1 < H:
            ahead = scores_of(h + 1)
        if h == 0:
            kt_scr[...] = dot_nt(wt_ref[E : 2 * E], nb).astype(bf16)
        if h == 3:
            ones = jnp.where((lane == E) | (lane == E + 1), 1.0, 0.0)
            va_scr[...] = (pad_lanes(dot_nt(nb, wt_ref[2 * E : 3 * E])) + ones).astype(bf16)
        if h == 4:
            q_cells = pad_lanes(dot_nt(nb_own, wt_ref[:E]).astype(bf16))
            for i in range(H):
                qm_scr[n * i : n * (i + 1), :] = jnp.where(head_lane == i, q_cells, 0)
        if h == 2:
            d_hidden = dot(own_ref[:, E:], wdown_ref[...])
        if h == 1:
            nb_t = transposed(nb).astype(bf16)
            cot_t = transposed(own_ref[:, E:]).astype(bf16)
        top = jnp.max(scores, axis=0, keepdims=True)
        e = jnp.exp2((scores - top) * EXP2_SCALE).astype(bf16)
        e_scr[:, n * h : n * (h + 1)] = e
        out = dot(jnp.concatenate([vt_scr[heads, :], one_rows], axis=0), e)
        inv = 1.0 / out[D : D + 1]
        inv_scr[8 * h : 8 * (h + 1), :] = jnp.broadcast_to(inv, (8, n))
        ot_scr[heads, :] = out[:D] * inv
    att_t = ot_scr[...]
    mid_b = (mid_own + dot(transposed(att_t).astype(bf16), wt_ref[3 * E :])).astype(bf16).astype(f32)
    normed_c, inv_c = norm(mid_b)
    nc = normed_c.astype(bf16)
    cot = own_ref[:, E:]
    pre = dot(nc, wup_ref[...])
    square = pre * pre
    half = 0.5 * jnp.tanh(pre * (GELU_A * GELU_B * square + GELU_A)) + 0.5
    smooth = pre * half
    hidden = smooth.astype(bf16)
    slope = half + (smooth - smooth * half) * (6.0 * GELU_A * GELU_B * square + 2.0 * GELU_A)
    d_pre = (d_hidden * slope).astype(bf16)
    lay_ref[...] = mid_b + dot_nt(hidden, wdown_ref[...])
    d_mid = cot.astype(f32) + norm_back(normed_c, inv_c, dot_nt(d_pre, wup_ref[...]))
    d_mid_low = d_mid.astype(bf16)
    d_att = dot_nt(wt_ref[3 * E :], d_mid_low).astype(bf16).astype(f32)
    d_low = []
    for h in range(H):
        heads = slice(D * h, D * (h + 1))
        d_low.append((d_att[heads] * inv_scr[8 * h : 8 * h + 1, :]).astype(bf16))

    def dprobs_of(h):
        heads = slice(D * h, D * (h + 1))
        delta = jnp.sum(d_low[h].astype(f32) * ot_scr[heads, :], axis=0, keepdims=True)
        return dot(va_scr[:, : E + 16], place(d_low[h], h, split_rows(delta)))

    ahead = dprobs_of(0)
    for h in range(H):
        heads = slice(D * h, D * (h + 1))
        dprobs = ahead
        if h + 1 < H:
            ahead = dprobs_of(h + 1)
        if h == 2:
            d_cells = pad_lanes(transposed(jnp.concatenate(d_low, axis=0)).astype(bf16))
            for i in range(H):
                dm_scr[n * i : n * (i + 1), :] = jnp.where(head_lane == i, d_cells, 0)
        if h == 4:
            sum_out = dot(att_t.astype(bf16), d_mid_low)
        if h == 1:
            nc_t = transposed(nc).astype(bf16)
        if h == 3:
            sum_up = dot(nc_t, d_pre).astype(bf16)
            sum_down = dot(cot_t, hidden).astype(bf16)
            for t in range(6):
                sums_scr[E * (6 + t) : E * (7 + t), :] = sum_up[:, 128 * t : 128 * (t + 1)]
                sums_scr[E * (12 + t) : E * (13 + t), :] = sum_down[:, 128 * t : 128 * (t + 1)]
        ds = (e_scr[:, n * h : n * (h + 1)].astype(f32) * dprobs).astype(bf16)
        ds_scr[:, n * h : n * (h + 1)] = ds
        dqt_scr[heads, :] = dot(kt_scr[heads, :], ds)
    dq = pad_lanes((transposed(dqt_scr[...]) * SCALE).astype(bf16))
    dk = (dot(ds_scr[...], qm_scr[...]) * SCALE).astype(bf16)
    dv = dot(e_scr[...], dm_scr[...]).astype(bf16)
    tiles = pack_tiles(dot(nb_t[:, :n], dq), dot(nb_t, dk), dot(nb_t, dv), pad_lanes(sum_out))
    for t in range(6):
        sums_scr[E * t : E * (t + 1), :] = tiles[t].astype(bf16)
    halve(core_ref, sums_scr, keep_ref, send_ref, EARLY)
    grad = dot(dk[:, :E], wt_ref[E : 2 * E]) + dot(dv[:, :E], wt_ref[2 * E : 3 * E])
    grad_own = grad[:n] + dot(dq[:, :E], wt_ref[:E])
    dmid_ref[...] = d_mid_low.astype(f32) + norm_back(normed_own, inv_own, grad_own)
    nsib_ref[...] = norm_back(normed_sib, inv_sib, grad[n:]).astype(bf16)


def sum_shares(parts_ref, out_ref):
    total = jnp.sum(parts_ref[...].astype(f32), axis=0).astype(bf16)
    out_ref[...] = jnp.broadcast_to(total[None], out_ref.shape)


def join(d_own_ref, n_recv_ref, lay_ref, keep_ref, recv_ref, out_ref, early_ref):
    d_mid = d_own_ref[...] + n_recv_ref[...].astype(f32)
    out_ref[...] = jnp.concatenate([d_mid, lay_ref[...]], axis=1).astype(bf16)
    early_ref[...] = (keep_ref[...].astype(f32) + recv_ref[...].astype(f32)).astype(bf16)


def merge(early_ref, keep_ref, recv_ref, out_ref):
    out_ref[:EARLY, :] = early_ref[...]
    out_ref[EARLY : EARLY + LATE, :] = (keep_ref[...].astype(f32) + recv_ref[...].astype(f32)).astype(bf16)
    out_ref[EARLY + LATE :, :] = jnp.zeros((SHARE - EARLY - LATE, 128), bf16)


def assemble(own_ref, back_ref, grad_ref):
    grad_ref[...] = (own_ref[...] + back_ref[...].astype(f32)).astype(bf16)


def finish(core_ref, own_ref, sib_ref, qkv_f_ref, out_f_ref, qkv_s_ref, out_s_ref, up_ref, down_ref, scr):
    core = core_ref[0]
    rows = EARLY + LATE
    scr[pl.ds(pl.multiple_of(core * rows, 64), rows), :] = own_ref[:rows, :]
    scr[pl.ds(pl.multiple_of((1 - core) * rows, 64), rows), :] = sib_ref[:rows, :]
    factor = 2.0 ** -8

    def early(t):
        at = E * t if t < 9 else E * t + LATE
        return scr[at : at + E, :].astype(f32)

    def late(t):
        at = EARLY + E * t if t < 3 else 2 * EARLY + E * t
        return scr[at : at + E, :].astype(f32)

    unpack_tiles(early, qkv_s_ref, out_s_ref, factor)
    unpack_tiles(late, qkv_f_ref, out_f_ref, factor)
    for t in range(6):
        up_ref[:, 128 * t : 128 * (t + 1)] = early(6 + t) * factor
        down_ref[:, 128 * t : 128 * (t + 1)] = early(12 + t) * factor


def call(kernel, outs, scratch=(), flops=0, smem=0, name=None, mib=12, in_hbm=0, out_hbm=0, sems=0):
    vmem = pl.BlockSpec(memory_space=pltpu.VMEM)
    hbm = pl.BlockSpec(memory_space=pltpu.HBM)

    def run(*args):
        in_specs = [pl.BlockSpec(memory_space=pltpu.SMEM)] * smem + [vmem] * (len(args) - smem - in_hbm) + [hbm] * in_hbm
        moved = sum(a.size * a.dtype.itemsize for a in args) if flops else 0
        return pl.pallas_call(
            kernel,
            out_shape=[jax.ShapeDtypeStruct(s, t) for s, t in outs],
            in_specs=in_specs,
            out_specs=[vmem] * (len(outs) - out_hbm) + [hbm] * out_hbm,
            scratch_shapes=[pltpu.VMEM(s, t) for s, t in scratch] + [pltpu.SemaphoreType.DMA((sems,))] * (sems > 0),
            compiler_params=pltpu.CompilerParams(vmem_limit_bytes=mib * 1024 * 1024),
            cost_estimate=pl.CostEstimate(flops=flops, bytes_accessed=moved, transcendentals=0),
            name=name,
        )(*args)

    return run


def shards(cells, split, w_qkv_feat, w_out_feat, w_qkv_samp, w_out_samp, w_up, w_down, cotangent):
    core = lax.axis_index("core")
    group = ("zhi", "chip")
    swap = [(0, 1), (1, 0)]
    wf_t = jnp.concatenate([w_qkv_feat.T, w_out_feat], axis=0)
    ws_t = jnp.concatenate([w_qkv_samp.T, w_out_samp], axis=0)
    core_arr = core.astype(jnp.int32).reshape(1)
    cells = cells.reshape(512, E)

    recv = lax.ppermute(cells, "zhi", swap)
    (mid,) = call(
        row_forward, [((512, 2 * E), bf16)], [((E, 512), f32)], flops=900_000_000, name="row_forward"
    )(cells, cotangent.reshape(512, E), recv, wf_t)

    train = jnp.arange(16, dtype=jnp.int32)[None, :] < split[:, None]
    bias = jnp.where(train, 0.0, NEG).astype(f32).reshape(32, 2, 16).transpose(1, 0, 2).reshape(2, 512)
    bias = jnp.where(core == 0, bias, bias[::-1]).reshape(1, 1024)
    bias = jnp.pad(bias, ((0, 15), (0, 0)))
    mid, bias, ws_t = lax.optimization_barrier((mid, bias, ws_t))
    own = lax.all_to_all(mid.reshape(32, 16, 2 * E), "chip", 0, 0, tiled=True).reshape(512, 2 * E)
    sib = lax.ppermute(own, "core", swap)

    lay, d_own, n_sib, early_keep, early_send = call(
        column,
        [((512, E), f32), ((512, E), f32), ((512, E), bf16), ((EARLY, 128), bf16), ((EARLY, 128), bf16)],
        [
            ((2 * EARLY, 128), bf16),
            ((1024, 256), bf16), ((1024, 256), bf16), ((E, 1024), bf16), ((E, 1024), bf16), ((E, 512), bf16),
            ((1024, H * 512), bf16), ((1024, H * 512), bf16), ((H * 512, 256), bf16), ((H * 512, 256), bf16),
            ((E, 512), f32), ((8 * H, 512), f32), ((E, 512), f32),
        ],
        flops=8_000_000_000, smem=1, name="column", mib=32,
    )(core_arr, own, sib, bias, ws_t, w_up, w_down.T)

    n_recv = lax.ppermute(n_sib, "core", swap)
    early_recv = lax.ppermute(early_send, "core", swap)
    joined, early = call(
        join, [((512, 2 * E), bf16), ((EARLY, 128), bf16)], flops=10_000_000, name="join"
    )(d_own, n_recv, lay, early_keep, early_recv)
    joined, recv = lax.optimization_barrier((joined, recv))
    rows = lax.all_to_all(joined.reshape(32, 16, 2 * E), "chip", 0, 0, tiled=True).reshape(512, 2 * E)

    saved = call(
        row_again,
        [
            ((E, 512), bf16), ((1024, E), bf16), ((E, 512), bf16), ((E, 1024), bf16), ((4, 2 * D, 768), bf16),
        ],
        [((E, 512), f32)],
        name="row_again",
    )(cells, recv, wf_t)

    layer_out, dmid, dq, dk, dv, late_keep, late_send = call(
        row_backward,
        [
            ((512, E), bf16), ((512, E), f32), ((512, 256), bf16), ((1024, 256), bf16), ((1024, 256), bf16),
            ((LATE, 128), bf16), ((LATE, 128), bf16),
        ],
        [((2 * LATE, 128), bf16), ((E, 512), f32), ((1024, E), f32), ((1024, E), f32)],
        flops=1_500_000_000, smem=1, name="row_backward",
    )(core_arr, rows, wf_t, *saved)
    late_recv = lax.ppermute(late_send, "core", swap)
    mine, other = call(
        cells_grad, [((512, E), f32), ((512, E), bf16)], flops=20_000_000_000, name="cells_grad"
    )(dmid, dq, dk, dv, cells, recv, wf_t)
    back = lax.ppermute(other, "zhi", swap)
    late_recv, mine = lax.optimization_barrier((late_recv, mine))
    (share,) = call(merge, [((SHARE, 128), bf16)], flops=100_000_000_000, name="merge")(early, late_keep, late_recv)
    parts = lax.all_to_all(share.reshape(64, CHUNK, 128), group, 0, 0, tiled=True)
    (grad_cells,) = call(assemble, [((512, E), bf16)], flops=100_000_000_000, name="assemble")(mine, back)
    parts, grad_cells = lax.optimization_barrier((parts, grad_cells))
    (total,) = call(sum_shares, [((64, CHUNK, 128), bf16)], flops=10_000_000, name="sum_shares")(parts)
    sums = lax.all_to_all(total, group, 0, 0, tiled=True).reshape(SHARE, 128)
    sums_sib = lax.ppermute(sums, "core", swap)
    g_qkv_feat, g_out_feat, g_qkv_samp, g_out_samp, g_up, g_down_t = call(
        finish,
        [((E, 576), f32), ((E, E), f32), ((E, 576), f32), ((E, E), f32), ((E, 768), f32), ((E, 768), f32)],
        [((2 * (EARLY + LATE), 128), bf16)],
        flops=10_000_000, smem=1, name="finish",
    )(core_arr, sums, sums_sib)
    return (
        layer_out.reshape(16, 32, E), grad_cells.reshape(16, 32, E),
        g_qkv_feat, g_out_feat, g_qkv_samp, g_out_samp, g_up, g_down_t.T,
    )


def solution(mesh):
    wide = Mesh(mesh.devices.reshape(32, 2, 2), ("chip", "core", "zhi"))
    cells = P(("chip", "core"), "zhi", None)
    return jax.shard_map(
        shards,
        mesh=wide,
        in_specs=(cells, P(), P(), P(), P(), P(), P(), P(), cells),
        out_specs=(cells, cells, P(), P(), P(), P(), P(), P()),
        check_vma=False,
    )
```

```python
import jax
import jax.numpy as jnp
from jax import lax
from jax.experimental import pallas as pl
from jax.experimental.pallas import tpu as pltpu
from jax.sharding import Mesh, PartitionSpec as P

H = 6
D = 32
E = 192
EPS = 1e-05
SCALE = D ** -0.5
EXP2_SCALE = SCALE * 1.4426950408889634
NEG = -1e30
GELU_A = 0.7978845608028654
GELU_B = 0.044715
f32 = jnp.float32
bf16 = jnp.bfloat16
EARLY = 9 * E
LATE = 3 * E
CHUNK = 40
SHARE = 64 * CHUNK


def dot(a, b):
    return jnp.dot(a, b, preferred_element_type=f32)


def dot_nt(a, b):
    return lax.dot_general(a, b, (((1,), (1,)), ((), ())), preferred_element_type=f32)


def transposed(v):
    return jnp.transpose(v)


def lane_mean(v):
    return dot(v.astype(bf16), jnp.full((E, E), 1.0, bf16)) * (1.0 / E)


def norm(v):
    centered = v - lane_mean(v)
    inv_std = lax.rsqrt(lane_mean(centered * centered) + EPS)
    return centered * inv_std, inv_std


def norm_back(normed, inv_std, grad):
    return inv_std * (grad - lane_mean(grad) - normed * lane_mean(grad * normed))


def place(rows, head, extra=None):
    count = rows.shape[1]
    parts = []
    if head > 0:
        parts.append(jnp.zeros((D * head, count), bf16))
    parts.append(rows)
    if head < H - 1:
        parts.append(jnp.zeros((E - D * (head + 1), count), bf16))
    if extra is not None:
        parts.append(extra)
    return jnp.concatenate(parts, axis=0)


def split_rows(delta):
    high = (-delta).astype(bf16).astype(f32)
    low = -delta - high
    at = lax.broadcasted_iota(jnp.int32, (16, delta.shape[1]), 0)
    return jnp.where(at == 0, high, jnp.where(at == 1, low, 0.0)).astype(bf16)


def pack_tiles(q, k, v, out):
    lane = lax.broadcasted_iota(jnp.int32, (E, 128), 1)
    roll = lambda t: pltpu.roll(t, 64, 1)
    low = lane < 64
    return (
        q[:, :128],
        jnp.where(low, q[:, 128:], roll(k[:, :128])),
        jnp.where(low, roll(k[:, :128]), roll(k[:, 128:])),
        v[:, :128],
        out[:, :128],
        jnp.where(low, v[:, 128:], roll(out[:, 128:])),
    )


def unpack_tiles(tile, qkv_ref, out_ref, factor):
    for t in range(4):
        qkv_ref[:, 128 * t : 128 * (t + 1)] = tile(t) * factor
    last = tile(5) * factor
    qkv_ref[:, 512:576] = last[:, :64]
    out_ref[:, :128] = tile(4) * factor
    out_ref[:, 128:192] = pltpu.roll(last, 64, 1)[:, :64]


def pad_lanes(v):
    return jnp.concatenate([v, jnp.zeros((v.shape[0], 256 - E), v.dtype)], axis=1)


def halve(core_ref, sums_scr, keep_ref, send_ref, rows):
    core = core_ref[0]
    keep_ref[...] = sums_scr[pl.ds(pl.multiple_of(core * rows, 64), rows), :]
    send_ref[...] = sums_scr[pl.ds(pl.multiple_of((1 - core) * rows, 64), rows), :]


def row_masks():
    row = (lax.broadcasted_iota(jnp.int32, (D, 128 * H), 1) // 32) % 4
    return [row == i for i in range(4)]


def same_row(masks, full):
    halves = []
    for at in (0, 128):
        part = full[at + 96 : at + 128]
        for i in range(3):
            part = jnp.where(masks[i], full[at + 32 * i : at + 32 * (i + 1)], part)
        halves.append(part)
    return jnp.concatenate(halves, axis=0)


def spread(masks, part):
    parts = [jnp.where(mask, part[at : at + D], 0.0) for at in (0, D) for mask in masks]
    return jnp.concatenate(parts, axis=0).astype(bf16)


def grouped(cells_ref, recv_ref):
    parts = [ref[128 * p : 128 * (p + 1), :] for p in range(4) for ref in (cells_ref, recv_ref)]
    return jnp.concatenate(parts, axis=0).astype(f32)


def own_lanes(v):
    return jnp.concatenate([v[:, 256 * p : 256 * p + 128] for p in range(4)], axis=1)


def attend(cells_ref, recv_ref, wt_ref, ot_ref, keep=None):
    masks = row_masks()
    one_rows = jnp.ones((16, 256), bf16)
    na = norm(grouped(cells_ref, recv_ref))[0].astype(bf16)
    qt = own_lanes(dot_nt(wt_ref[:E], na).astype(bf16))
    keys = dot_nt(na, wt_ref[E : 2 * E]).astype(bf16)
    vt = dot_nt(wt_ref[2 * E : 3 * E], na).astype(bf16)
    if keep is not None:
        na_ref, kt_ref, p_ref = keep
        na_ref[...] = na
        kt_ref[...] = dot_nt(wt_ref[E : 2 * E], na).astype(bf16)
    for p in range(4):
        cols = slice(128 * p, 128 * (p + 1))
        both = slice(256 * p, 256 * (p + 1))
        rhs = jnp.concatenate([place(qt[D * h : D * (h + 1), cols], h) for h in range(H)], axis=1)
        scores = same_row(masks, dot(keys[both], rhs))
        e = jnp.exp2((scores - jnp.max(scores, axis=0, keepdims=True)) * EXP2_SCALE)
        wide_e = spread(masks, e)
        invs = []
        for h in range(H):
            heads = slice(D * h, D * (h + 1))
            wide = slice(128 * h, 128 * (h + 1))
            out = dot(jnp.concatenate([vt[heads, both], one_rows], axis=0), wide_e[:, wide])
            inv = 1.0 / out[D : D + 1]
            invs.append(inv)
            ot_ref[heads, cols] = out[:D] * inv
        if keep is not None:
            p_ref[p] = (e * jnp.concatenate(invs, axis=1)).astype(bf16)


def row_forward(cells_ref, cot_ref, recv_ref, wt_ref, mid_ref, ot_scr):
    attend(cells_ref, recv_ref, wt_ref, ot_scr)
    mid = cells_ref[...].astype(f32) + dot(transposed(ot_scr[...]).astype(bf16), wt_ref[3 * E :])
    both = jnp.concatenate([mid, cot_ref[...].astype(f32)], axis=1).reshape(16, 32, 2 * E)
    mid_ref[...] = jnp.swapaxes(both, 0, 1).reshape(512, 2 * E).astype(bf16)


def row_again(cells_ref, recv_ref, wt_ref, ot_ref, *rest):
    keep, ot_scr = rest[:-1], rest[-1]
    attend(cells_ref, recv_ref, wt_ref, ot_scr, keep)
    ot_ref[...] = ot_scr[...].astype(bf16)


def row_backward(
    core_ref, rows_ref, wt_ref, ot_ref, na_ref, kt_ref, p_ref,
    lay_ref, dmid_ref, dq_ref, dk_ref, dv_ref, keep_ref, send_ref, sums_scr, dqt_scr, dk_scr, dv_scr,
):
    both = jnp.swapaxes(rows_ref[...].astype(f32).reshape(32, 16, 2 * E), 0, 1).reshape(512, 2 * E)
    lay_ref[...] = both[:, E:].astype(bf16)
    dmid_ref[...] = both[:, :E]
    dmid_low = both[:, :E].astype(bf16)
    d_att = dot_nt(wt_ref[3 * E :], dmid_low).astype(bf16)
    na = na_ref[...]
    own = jnp.concatenate([na[256 * p : 256 * p + 128] for p in range(4)], axis=0)
    qt = dot_nt(wt_ref[:E], own).astype(bf16)
    lane = lax.broadcasted_iota(jnp.int32, (1024, 256), 1)
    ones = jnp.where((lane == E) | (lane == E + 1), 1.0, 0.0)
    va = (pad_lanes(dot_nt(na, wt_ref[2 * E : 3 * E])) + ones).astype(bf16)
    masks = row_masks()
    for p in range(4):
        cols = slice(128 * p, 128 * (p + 1))
        both = slice(256 * p, 256 * (p + 1))
        blocks = []
        for h in range(H):
            heads = slice(D * h, D * (h + 1))
            d_out = d_att[heads, cols]
            delta = jnp.sum(d_out.astype(f32) * ot_ref[heads, cols].astype(f32), axis=0, keepdims=True)
            blocks.append(place(d_out, h, split_rows(delta)))
        rhs = jnp.concatenate(blocks, axis=1)
        q_rhs = jnp.concatenate([place(qt[D * h : D * (h + 1), cols], h) for h in range(H)], axis=1)
        if p == 0:
            na_t = transposed(na).astype(bf16)
        if p == 2:
            sum_out = dot(ot_ref[...], dmid_low)
        part = p_ref[p].astype(f32)
        ds = spread(masks, part * same_row(masks, dot(va[both, : E + 16], rhs)))
        dk_scr[both, :] = dot_nt(ds, q_rhs)
        dv_scr[both, :] = dot_nt(spread(masks, part), rhs[:E])
        for h in range(H):
            heads = slice(D * h, D * (h + 1))
            dqt_scr[heads, cols] = dot(kt_ref[heads, both], ds[:, 128 * h : 128 * (h + 1)])
    dq = pad_lanes((transposed(dqt_scr[...]) * SCALE).astype(bf16))
    dk = pad_lanes((dk_scr[...] * SCALE).astype(bf16))
    dv = pad_lanes(dv_scr[...].astype(bf16))
    dq_ref[...] = dq
    dk_ref[...] = dk
    dv_ref[...] = dv
    tiles = pack_tiles(dot(own_lanes(na_t), dq), dot(na_t, dk), dot(na_t, dv), pad_lanes(sum_out))
    for t in range(6):
        sums_scr[E * t : E * (t + 1), :] = tiles[t].astype(bf16)
    halve(core_ref, sums_scr, keep_ref, send_ref, LATE)


def cells_grad(dmid_ref, dq_ref, dk_ref, dv_ref, cells_ref, recv_ref, wt_ref, own_ref, other_ref):
    grad = dot(dk_ref[:, :E], wt_ref[E : 2 * E]) + dot(dv_ref[:, :E], wt_ref[2 * E : 3 * E])
    split = [jnp.concatenate([grad[256 * p + at : 256 * p + at + 128] for p in range(4)], axis=0) for at in (0, 128)]
    normed, inv_std = norm(recv_ref[...].astype(f32))
    other_ref[...] = norm_back(normed, inv_std, split[1]).astype(bf16)
    normed, inv_std = norm(cells_ref[...].astype(f32))
    own_ref[...] = dmid_ref[...] + norm_back(normed, inv_std, split[0] + dot(dq_ref[:, :E], wt_ref[:E]))


def column(
    core_ref, own_ref, sib_ref, bias_ref, wt_ref, wup_ref, wdown_ref,
    lay_ref, dmid_ref, nsib_ref, keep_ref, send_ref,
    sums_scr, ka_scr, va_scr, vt_scr, kt_scr, qt_scr, e_scr, ds_scr, qm_scr, dm_scr, ot_scr, inv_scr, dqt_scr,
):
    n = 512
    mid_own = own_ref[:, :E].astype(f32)
    normed_own, inv_own = norm(mid_own)
    normed_sib, inv_sib = norm(sib_ref[:, :E].astype(f32))
    nb_own = normed_own.astype(bf16)
    nb = jnp.concatenate([nb_own, normed_sib.astype(bf16)], axis=0)
    lane = lax.broadcasted_iota(jnp.int32, (2 * n, 256), 1)
    at = lax.broadcasted_iota(jnp.int32, (16, 256), 0)
    col = lax.broadcasted_iota(jnp.int32, (16, 256), 1)
    place_bias = jnp.where((at == 0) & (col == E), 1.0, 0.0).astype(bf16)
    bias = dot(jnp.transpose(bias_ref[...]).astype(bf16), place_bias)
    ka_scr[...] = (pad_lanes(dot_nt(nb, wt_ref[E : 2 * E])) + bias).astype(bf16)
    qt_scr[...] = dot_nt(wt_ref[:E], nb_own).astype(bf16)
    vt_scr[...] = dot_nt(wt_ref[2 * E : 3 * E], nb).astype(bf16)
    one_rows = jnp.ones((16, 2 * n), bf16)
    at = lax.broadcasted_iota(jnp.int32, (16, n), 0)
    extra = jnp.where(at == 0, 1.0, 0.0).astype(bf16)
    head_lane = lax.broadcasted_iota(jnp.int32, (n, 256), 1) // D

    def scores_of(h):
        return dot(ka_scr[:, : E + 16], place(qt_scr[D * h : D * (h + 1), :], h, extra))

    ahead = scores_of(0)
    for h in range(H):
        heads = slice(D * h, D * (h + 1))
        scores = ahead
        if h + 1 < H:
            ahead = scores_of(h + 1)
        if h == 0:
            kt_scr[...] = dot_nt(wt_ref[E : 2 * E], nb).astype(bf16)
        if h == 3:
            ones = jnp.where((lane == E) | (lane == E + 1), 1.0, 0.0)
            va_scr[...] = (pad_lanes(dot_nt(nb, wt_ref[2 * E : 3 * E])) + ones).astype(bf16)
        if h == 4:
            q_cells = pad_lanes(dot_nt(nb_own, wt_ref[:E]).astype(bf16))
            for i in range(H):
                qm_scr[n * i : n * (i + 1), :] = jnp.where(head_lane == i, q_cells, 0)
        if h == 2:
            d_hidden = dot(own_ref[:, E:], wdown_ref[...])
        if h == 1:
            nb_t = transposed(nb).astype(bf16)
            cot_t = transposed(own_ref[:, E:]).astype(bf16)
        top = jnp.max(scores, axis=0, keepdims=True)
        e = jnp.exp2((scores - top) * EXP2_SCALE).astype(bf16)
        e_scr[:, n * h : n * (h + 1)] = e
        out = dot(jnp.concatenate([vt_scr[heads, :], one_rows], axis=0), e)
        inv = 1.0 / out[D : D + 1]
        inv_scr[8 * h : 8 * (h + 1), :] = jnp.broadcast_to(inv, (8, n))
        ot_scr[heads, :] = out[:D] * inv
    att_t = ot_scr[...]
    mid_b = (mid_own + dot(transposed(att_t).astype(bf16), wt_ref[3 * E :])).astype(bf16).astype(f32)
    normed_c, inv_c = norm(mid_b)
    nc = normed_c.astype(bf16)
    cot = own_ref[:, E:]
    pre = dot(nc, wup_ref[...])
    square = pre * pre
    half = 0.5 * jnp.tanh(pre * (GELU_A * GELU_B * square + GELU_A)) + 0.5
    smooth = pre * half
    hidden = smooth.astype(bf16)
    slope = half + (smooth - smooth * half) * (6.0 * GELU_A * GELU_B * square + 2.0 * GELU_A)
    d_pre = (d_hidden * slope).astype(bf16)
    lay_ref[...] = mid_b + dot_nt(hidden, wdown_ref[...])
    d_mid = cot.astype(f32) + norm_back(normed_c, inv_c, dot_nt(d_pre, wup_ref[...]))
    d_mid_low = d_mid.astype(bf16)
    d_att = dot_nt(wt_ref[3 * E :], d_mid_low).astype(bf16).astype(f32)
    d_low = []
    for h in range(H):
        heads = slice(D * h, D * (h + 1))
        d_low.append((d_att[heads] * inv_scr[8 * h : 8 * h + 1, :]).astype(bf16))

    def dprobs_of(h):
        heads = slice(D * h, D * (h + 1))
        delta = jnp.sum(d_low[h].astype(f32) * ot_scr[heads, :], axis=0, keepdims=True)
        return dot(va_scr[:, : E + 16], place(d_low[h], h, split_rows(delta)))

    ahead = dprobs_of(0)
    for h in range(H):
        heads = slice(D * h, D * (h + 1))
        dprobs = ahead
        if h + 1 < H:
            ahead = dprobs_of(h + 1)
        if h == 2:
            d_cells = pad_lanes(transposed(jnp.concatenate(d_low, axis=0)).astype(bf16))
            for i in range(H):
                dm_scr[n * i : n * (i + 1), :] = jnp.where(head_lane == i, d_cells, 0)
        if h == 5:
            dv = dot(e_scr[...], dm_scr[...]).astype(bf16)
        if h == 4:
            sum_out = dot(att_t.astype(bf16), d_mid_low)
        if h == 1:
            nc_t = transposed(nc).astype(bf16)
        if h == 3:
            sum_up = dot(nc_t, d_pre).astype(bf16)
            sum_down = dot(cot_t, hidden).astype(bf16)
            for t in range(6):
                sums_scr[E * (6 + t) : E * (7 + t), :] = sum_up[:, 128 * t : 128 * (t + 1)]
                sums_scr[E * (12 + t) : E * (13 + t), :] = sum_down[:, 128 * t : 128 * (t + 1)]
        ds = (e_scr[:, n * h : n * (h + 1)].astype(f32) * dprobs).astype(bf16)
        ds_scr[:, n * h : n * (h + 1)] = ds
        dqt_scr[heads, :] = dot(kt_scr[heads, :], ds)
    dq = pad_lanes((transposed(dqt_scr[...]) * SCALE).astype(bf16))
    dk = (dot(ds_scr[...], qm_scr[...]) * SCALE).astype(bf16)
    tiles = pack_tiles(dot(nb_t[:, :n], dq), dot(nb_t, dk), dot(nb_t, dv), pad_lanes(sum_out))
    for t in range(6):
        sums_scr[E * t : E * (t + 1), :] = tiles[t].astype(bf16)
    halve(core_ref, sums_scr, keep_ref, send_ref, EARLY)
    grad = dot(dk[:, :E], wt_ref[E : 2 * E]) + dot(dv[:, :E], wt_ref[2 * E : 3 * E])
    grad_own = grad[:n] + dot(dq[:, :E], wt_ref[:E])
    dmid_ref[...] = d_mid_low.astype(f32) + norm_back(normed_own, inv_own, grad_own)
    nsib_ref[...] = norm_back(normed_sib, inv_sib, grad[n:]).astype(bf16)


def sum_shares(parts_ref, out_ref):
    total = jnp.sum(parts_ref[...].astype(f32), axis=0).astype(bf16)
    out_ref[...] = jnp.broadcast_to(total[None], out_ref.shape)


def join(d_own_ref, n_recv_ref, lay_ref, out_ref):
    d_mid = d_own_ref[...] + n_recv_ref[...].astype(f32)
    out_ref[...] = jnp.concatenate([d_mid, lay_ref[...]], axis=1).astype(bf16)


def early_add(keep_ref, recv_ref, early_ref):
    early_ref[...] = (keep_ref[...].astype(f32) + recv_ref[...].astype(f32)).astype(bf16)


def merge(early_ref, keep_ref, recv_ref, out_ref):
    out_ref[:EARLY, :] = early_ref[...]
    out_ref[EARLY : EARLY + LATE, :] = (keep_ref[...].astype(f32) + recv_ref[...].astype(f32)).astype(bf16)
    out_ref[EARLY + LATE :, :] = jnp.zeros((SHARE - EARLY - LATE, 128), bf16)


def assemble(own_ref, back_ref, grad_ref):
    grad_ref[...] = (own_ref[...] + back_ref[...].astype(f32)).astype(bf16)


def finish(core_ref, own_ref, sib_ref, qkv_f_ref, out_f_ref, qkv_s_ref, out_s_ref, up_ref, down_ref, scr):
    core = core_ref[0]
    rows = EARLY + LATE
    scr[pl.ds(pl.multiple_of(core * rows, 64), rows), :] = own_ref[:rows, :]
    scr[pl.ds(pl.multiple_of((1 - core) * rows, 64), rows), :] = sib_ref[:rows, :]
    factor = 2.0 ** -8

    def early(t):
        at = E * t if t < 9 else E * t + LATE
        return scr[at : at + E, :].astype(f32)

    def late(t):
        at = EARLY + E * t if t < 3 else 2 * EARLY + E * t
        return scr[at : at + E, :].astype(f32)

    unpack_tiles(early, qkv_s_ref, out_s_ref, factor)
    unpack_tiles(late, qkv_f_ref, out_f_ref, factor)
    for t in range(6):
        up_ref[:, 128 * t : 128 * (t + 1)] = early(6 + t) * factor
        down_ref[:, 128 * t : 128 * (t + 1)] = early(12 + t) * factor


def call(kernel, outs, scratch=(), flops=0, smem=0, name=None, mib=12, in_hbm=0, out_hbm=0, sems=0):
    vmem = pl.BlockSpec(memory_space=pltpu.VMEM)
    hbm = pl.BlockSpec(memory_space=pltpu.HBM)

    def run(*args):
        in_specs = [pl.BlockSpec(memory_space=pltpu.SMEM)] * smem + [vmem] * (len(args) - smem - in_hbm) + [hbm] * in_hbm
        moved = sum(a.size * a.dtype.itemsize for a in args) if flops else 0
        return pl.pallas_call(
            kernel,
            out_shape=[jax.ShapeDtypeStruct(s, t) for s, t in outs],
            in_specs=in_specs,
            out_specs=[vmem] * (len(outs) - out_hbm) + [hbm] * out_hbm,
            scratch_shapes=[pltpu.VMEM(s, t) for s, t in scratch] + [pltpu.SemaphoreType.DMA((sems,))] * (sems > 0),
            compiler_params=pltpu.CompilerParams(vmem_limit_bytes=mib * 1024 * 1024),
            cost_estimate=pl.CostEstimate(flops=flops, bytes_accessed=moved, transcendentals=0),
            name=name,
        )(*args)

    return run


def shards(cells, split, w_qkv_feat, w_out_feat, w_qkv_samp, w_out_samp, w_up, w_down, cotangent):
    core = lax.axis_index("core")
    group = ("zhi", "chip")
    swap = [(0, 1), (1, 0)]
    wf_t = jnp.concatenate([w_qkv_feat.T, w_out_feat], axis=0)
    ws_t = jnp.concatenate([w_qkv_samp.T, w_out_samp], axis=0)
    core_arr = core.astype(jnp.int32).reshape(1)
    cells = cells.reshape(512, E)

    recv = lax.ppermute(cells, "zhi", swap)
    (mid,) = call(
        row_forward, [((512, 2 * E), bf16)], [((E, 512), f32)], flops=900_000_000, name="row_forward"
    )(cells, cotangent.reshape(512, E), recv, wf_t)

    train = jnp.arange(16, dtype=jnp.int32)[None, :] < split[:, None]
    bias = jnp.where(train, 0.0, NEG).astype(f32).reshape(32, 2, 16).transpose(1, 0, 2).reshape(2, 512)
    bias = jnp.where(core == 0, bias, bias[::-1]).reshape(1, 1024)
    bias = jnp.pad(bias, ((0, 15), (0, 0)))
    mid, bias, ws_t = lax.optimization_barrier((mid, bias, ws_t))
    own = lax.all_to_all(mid.reshape(32, 16, 2 * E), "chip", 0, 0, tiled=True).reshape(512, 2 * E)
    sib = lax.ppermute(own, "core", swap)

    lay, d_own, n_sib, early_keep, early_send = call(
        column,
        [((512, E), f32), ((512, E), f32), ((512, E), bf16), ((EARLY, 128), bf16), ((EARLY, 128), bf16)],
        [
            ((2 * EARLY, 128), bf16),
            ((1024, 256), bf16), ((1024, 256), bf16), ((E, 1024), bf16), ((E, 1024), bf16), ((E, 512), bf16),
            ((1024, H * 512), bf16), ((1024, H * 512), bf16), ((H * 512, 256), bf16), ((H * 512, 256), bf16),
            ((E, 512), f32), ((8 * H, 512), f32), ((E, 512), f32),
        ],
        flops=8_000_000_000, smem=1, name="column", mib=32,
    )(core_arr, own, sib, bias, ws_t, w_up, w_down.T)

    n_recv = lax.ppermute(n_sib, "core", swap)
    (joined,) = call(join, [((512, 2 * E), bf16)], flops=10_000_000, name="join")(d_own, n_recv, lay)
    joined, recv, early_send = lax.optimization_barrier((joined, recv, early_send))
    rows = lax.all_to_all(joined.reshape(32, 16, 2 * E), "chip", 0, 0, tiled=True).reshape(512, 2 * E)

    early_recv = lax.ppermute(early_send, "core", swap)
    (early,) = call(early_add, [((EARLY, 128), bf16)], name="early_add")(early_keep, early_recv)
    early, recv = lax.optimization_barrier((early, recv))
    saved = call(
        row_again,
        [
            ((E, 512), bf16), ((1024, E), bf16), ((E, 1024), bf16), ((4, 2 * D, 768), bf16),
        ],
        [((E, 512), f32)],
        name="row_again",
    )(cells, recv, wf_t)

    layer_out, dmid, dq, dk, dv, late_keep, late_send = call(
        row_backward,
        [
            ((512, E), bf16), ((512, E), f32), ((512, 256), bf16), ((1024, 256), bf16), ((1024, 256), bf16),
            ((LATE, 128), bf16), ((LATE, 128), bf16),
        ],
        [((2 * LATE, 128), bf16), ((E, 512), f32), ((1024, E), f32), ((1024, E), f32)],
        flops=1_500_000_000, smem=1, name="row_backward",
    )(core_arr, rows, wf_t, *saved)
    late_recv = lax.ppermute(late_send, "core", swap)
    mine, other = call(
        cells_grad, [((512, E), f32), ((512, E), bf16)], flops=20_000_000_000, name="cells_grad"
    )(dmid, dq, dk, dv, cells, recv, wf_t)
    back = lax.ppermute(other, "zhi", swap)
    late_recv, mine = lax.optimization_barrier((late_recv, mine))
    (share,) = call(merge, [((SHARE, 128), bf16)], flops=100_000_000_000, name="merge")(early, late_keep, late_recv)
    parts = lax.all_to_all(share.reshape(64, CHUNK, 128), group, 0, 0, tiled=True)
    (grad_cells,) = call(assemble, [((512, E), bf16)], flops=100_000_000_000, name="assemble")(mine, back)
    parts, grad_cells = lax.optimization_barrier((parts, grad_cells))
    (total,) = call(sum_shares, [((64, CHUNK, 128), bf16)], flops=10_000_000, name="sum_shares")(parts)
    sums = lax.all_to_all(total, group, 0, 0, tiled=True).reshape(SHARE, 128)
    sums_sib = lax.ppermute(sums, "core", swap)
    g_qkv_feat, g_out_feat, g_qkv_samp, g_out_samp, g_up, g_down_t = call(
        finish,
        [((E, 576), f32), ((E, E), f32), ((E, 576), f32), ((E, E), f32), ((E, 768), f32), ((E, 768), f32)],
        [((2 * (EARLY + LATE), 128), bf16)],
        flops=10_000_000, smem=1, name="finish",
    )(core_arr, sums, sums_sib)
    return (
        layer_out.reshape(16, 32, E), grad_cells.reshape(16, 32, E),
        g_qkv_feat, g_out_feat, g_qkv_samp, g_out_samp, g_up, g_down_t.T,
    )


def solution(mesh):
    wide = Mesh(mesh.devices.reshape(32, 2, 2), ("chip", "core", "zhi"))
    cells = P(("chip", "core"), "zhi", None)
    return jax.shard_map(
        shards,
        mesh=wide,
        in_specs=(cells, P(), P(), P(), P(), P(), P(), P(), cells),
        out_specs=(cells, cells, P(), P(), P(), P(), P(), P()),
        check_vma=False,
    )
```
